512 devices in a mesh: seq: 32 (over z, x_hi, core), ctx: 16 (over x_lo, y).
Axes of the slice: x: 4 (x_hi: 2, x_lo: 2; x = x_hi * 2 + x_lo), y: 8, z: 8, core: 2. Of those that a mesh axis runs over, the one named last changes fastest.
Arguments:
- queries: bfloat16 [32, 2048, 8192], P('seq', 'ctx'), may hold values from -6 to 6
- keys: bfloat16 [32, 2048, 1024], P('seq', 'ctx'), may hold values from -6 to 6
- doc_ids: int32 [32, 2048], P('seq'), may hold values from 0 to 2, never falling along the last dimension, each value on 1 to 1792 neighbouring positions
- gate_query_weight: bfloat16 [8192, 1024], P('ctx'), may hold values from -1 to 1
- gate_key_weight: bfloat16 [1024, 1024], P('ctx'), may hold values from -1 to 1
Outputs:
- grad_query_weight: bfloat16 [8192, 1024], P('ctx')
- grad_key_weight: bfloat16 [1024, 1024], P('ctx')
The draws below stay inside these ranges and needn't reach their ends.
Inputs may be any that keep to these rules, and one draw needn't show every extreme that they name: `doc_ids`: document ids of a sequence never fall, there are 3 documents, each of at most 1792 tokens, one exactly that long.
All inputs are finite; a program needn't handle non-finite values.
Results may differ from the reference program's by a relative error of at most 0.012.
The reference program's roundings to bfloat16 on the way (of `grad_gate_q` and `grad_gate_k`) count: a program that leaves them out, or rounds other values in their place, can miss the bound.
Values may be sent and summed in bfloat16 or wider, within the bound.
No kernel may reach another device: no remote copies, remote signals or barrier semaphores. Data moves between devices by JAX's collectives and lax.ppermute only.
A program may use at most 64 MiB of HBM per device.

```python
import math
import jax
import jax.numpy as jnp
import numpy as np
from jax import lax

HEADS = 64
KV_HEADS = 8
HEAD_DIM = 128
GATE_DIM = 128
BLOCK = 64
DOCS = 3
QW = 8192
KW = 1024
GW = 1024
SEQ_LEN = 2048
SEQS = 32


def draw_queries(key, part):
    key = jax.random.fold_in(key, 11)
    base_key = jax.random.fold_in(key, 0)
    full_shape = (SEQS, SEQ_LEN, QW)
    values = jax.random.truncated_normal(base_key, -6.0, 6.0, full_shape, jnp.float32)
    return values.astype(jnp.bfloat16)


def draw_keys(key, part):
    key = jax.random.fold_in(key, 12)
    full_shape = (SEQS, SEQ_LEN, KW)
    values = jax.random.truncated_normal(key, -6.0, 6.0, full_shape, jnp.float32)
    return values.astype(jnp.bfloat16)


def draw_gate_query_weight(key, part):
    key = jax.random.fold_in(key, 13)
    values = jax.random.truncated_normal(key, -6.0, 6.0, (QW, GW), jnp.float32) / math.sqrt(QW)
    return values.astype(jnp.bfloat16)


def draw_gate_key_weight(key, part):
    key = jax.random.fold_in(key, 14)
    values = jax.random.truncated_normal(key, -6.0, 6.0, (KW, GW), jnp.float32) / math.sqrt(KW)
    return values.astype(jnp.bfloat16)


def split_up(amount, total, most, skew):
    portions = [(1 << 20) // math.isqrt(grade ** skew) + 1 for grade in range(2, amount + 1)]
    spare, counts = total - most - (amount - 1), [1] * (amount - 1)
    while spare > 0:
        free = [i for i in range(amount - 1) if counts[i] < most]
        mass, remaining = sum([portions[i] for i in free]), spare
        for i in free:
            more = min(most - counts[i], max(1, remaining * portions[i] // mass), spare)
            counts[i] = counts[i] + more
            spare = spare - more
    return np.array([most] + counts)


def ragged(rng, number_of, total, reach, skew):
    if number_of == 2:
        one = jax.random.randint(rng, (), max(1, total - reach), min(reach, total - 1) + 1)
        return jnp.stack([one, total - one])
    sizes = jnp.asarray(split_up(number_of, total, reach, skew), jnp.int32)
    twos = (number_of - 1) // 2
    donor, receiver = sizes[1:1 + 2 * twos:2], sizes[2:2 + 2 * twos:2]
    room = jnp.minimum(donor - 1, reach - receiver)
    passed = jax.random.randint(jax.random.fold_in(rng, 1), (twos,), 0, 1 << 20) % (room + 1)
    sizes = sizes.at[1:1 + 2 * twos:2].set(donor - passed).at[2:2 + 2 * twos:2].set(receiver + passed)
    return sizes[jax.random.permutation(jax.random.fold_in(rng, 2), number_of)]


def setup_inputs(seed: int = 0) -> dict:
    arg_keys = jax.random.split(jax.random.key(seed), 6)
    queries = draw_queries(jax.random.fold_in(arg_keys[5], 71), 0)
    keys = draw_keys(jax.random.fold_in(arg_keys[5], 71), 0)
    doc_ids = jax.vmap(lambda own: jnp.searchsorted(jnp.cumsum(ragged(own, DOCS, SEQ_LEN, SEQ_LEN * 7 // 8, 0)), jnp.arange(SEQ_LEN), side="right"))(jax.random.split(arg_keys[2], SEQS)).reshape((SEQS, SEQ_LEN)).astype(jnp.int32)
    gate_query_weight = draw_gate_query_weight(jax.random.fold_in(arg_keys[5], 71), 0)
    gate_key_weight = draw_gate_key_weight(jax.random.fold_in(arg_keys[5], 71), 0)
    return dict(queries=queries, keys=keys, doc_ids=doc_ids, gate_query_weight=gate_query_weight, gate_key_weight=gate_key_weight)


NEG_FILL = -1.0e30


def seq_grads(query_rows, key_rows, doc_all, gate_query_weight, gate_key_weight):
    seq_len = query_rows.shape[0]
    num_blocks = seq_len // BLOCK
    group_size = HEADS // KV_HEADS
    attn_scale = 1.0 / (HEAD_DIM ** 0.5)
    gate_scale = 1.0 / (GATE_DIM ** 0.5)
    position = jnp.arange(seq_len, dtype=jnp.int32)
    visible = (position[None, :] <= position[:, None]) & (doc_all[None, :] == doc_all[:, None])

    def head_map(head_idx):
        kv_index = head_idx // group_size
        head_q = lax.dynamic_slice_in_dim(query_rows, (head_idx * HEAD_DIM).astype(jnp.int32), HEAD_DIM, 1)
        head_k = lax.dynamic_slice_in_dim(key_rows, (kv_index * HEAD_DIM).astype(jnp.int32), HEAD_DIM, 1)
        scores = lax.dot_general(head_q, head_k, (((1,), (1,)), ((), ())), preferred_element_type=jnp.float32) * attn_scale
        scores = jnp.where(visible, scores, NEG_FILL)
        peak = jnp.max(scores, axis=1, keepdims=True)
        total = jnp.sum(jnp.where(visible, jnp.exp(scores - peak), 0.0), axis=1, keepdims=True)
        lse = peak + jnp.log(total)
        prob = jnp.where(visible, jnp.exp(scores - lse), 0.0)
        return prob.reshape(num_blocks, BLOCK, num_blocks, BLOCK).max(axis=(1, 3))

    head_probs = lax.map(head_map, jnp.arange(HEADS, dtype=jnp.int32))
    raw_target = head_probs.reshape(KV_HEADS, group_size, num_blocks, num_blocks).sum(axis=1)
    target = raw_target / jnp.sum(raw_target, axis=-1, keepdims=True)

    pool_q = (jnp.sum(query_rows.reshape(num_blocks, BLOCK, -1).astype(jnp.float32), axis=1) / BLOCK).astype(jnp.bfloat16)
    pool_k = jnp.max(key_rows.reshape(num_blocks, BLOCK, -1), axis=1)
    gate_q = jnp.dot(pool_q, gate_query_weight, preferred_element_type=jnp.float32).astype(jnp.bfloat16)
    gate_k = jnp.dot(pool_k, gate_key_weight, preferred_element_type=jnp.float32).astype(jnp.bfloat16)
    gq_heads = gate_q.reshape(num_blocks, KV_HEADS, GATE_DIM).astype(jnp.float32)
    gk_heads = gate_k.reshape(num_blocks, KV_HEADS, GATE_DIM).astype(jnp.float32)
    logits = jnp.einsum("ahe,bhe->hab", gq_heads, gk_heads, precision=lax.Precision.HIGHEST) * gate_scale
    block_idx = jnp.arange(num_blocks, dtype=jnp.int32)
    causal = block_idx[None, :] <= block_idx[:, None]
    masked = jnp.where(causal, logits, NEG_FILL)
    peak = jnp.max(masked, axis=-1, keepdims=True)
    weights = jnp.where(causal, jnp.exp(masked - peak), 0.0)
    gate_prob = weights / jnp.sum(weights, axis=-1, keepdims=True)
    score_grad = jnp.where(causal, gate_prob - target, 0.0)
    grad_gate_q = (jnp.einsum("hab,bhe->ahe", score_grad, gk_heads, precision=lax.Precision.HIGHEST) * gate_scale).astype(jnp.bfloat16)
    grad_gate_k = (jnp.einsum("hab,ahe->bhe", score_grad, gq_heads, precision=lax.Precision.HIGHEST) * gate_scale).astype(jnp.bfloat16)
    grad_q = jnp.dot(pool_q.T, grad_gate_q.reshape(num_blocks, -1), preferred_element_type=jnp.float32)
    grad_k = jnp.dot(pool_k.T, grad_gate_k.reshape(num_blocks, -1), preferred_element_type=jnp.float32)
    return grad_q, grad_k


def reference(queries, keys, doc_ids, gate_query_weight, gate_key_weight):
    def absorb(running, inputs):
        grad_q, grad_k = seq_grads(inputs[0], inputs[1], inputs[2], gate_query_weight, gate_key_weight)
        return (running[0] + grad_q, running[1] + grad_k), None

    init = (jnp.zeros(gate_query_weight.shape, jnp.float32), jnp.zeros(gate_key_weight.shape, jnp.float32))
    totals, _ = lax.scan(absorb, init, (queries, keys, doc_ids))
    return totals[0].astype(jnp.bfloat16), totals[1].astype(jnp.bfloat16)
```

```python
import functools
import math

import jax
import jax.numpy as jnp
from jax import lax
from jax.experimental import pallas as pl
from jax.experimental.pallas import tpu as pltpu
from jax.sharding import Mesh, PartitionSpec as P

HEADS = 64
KV_HEADS = 8
GROUP = 8
HEAD_DIM = 128
GATE_DIM = 128
BLOCK = 64
SHARD = 128
TILE = 256
LOCAL_KV = 4
NUM_BLOCKS = 32
SEQ_AXES = ("z", "xh", "co")
CTX_AXES = ("xl", "y")
SWAP = [(0, 1), (1, 0)]
NEG_FILL = -1e30
EXP2_SCALE = math.log2(math.e) / math.sqrt(HEAD_DIM)


def attention_kernel(sc, q_own, q_recv, k_ref, out_ref, bias_s, m_s, l_s, bm_s, acc_s):
    h = pl.program_id(0)
    n0, n1, xl, y = sc[0], sc[1], sc[2], sc[3]
    lane = lax.broadcasted_iota(jnp.int32, (NUM_BLOCKS, 128), 1)

    @pl.when(h == 0)
    def _():
        acc_s[...] = jnp.zeros_like(acc_s)

    for rs, q_ref in enumerate((q_own, q_recv)):
        half = xl if rs == 0 else 1 - xl
        rank = half * 8 + y
        row0 = rank * SHARD
        first = jnp.where(row0 >= n1, n1, jnp.where(row0 >= n0, n0, 0))
        t_lo = first // TILE
        t_hi = rank // 2 + 1

        @pl.when(h == 0)
        def _():
            rowpos = row0 + lax.broadcasted_iota(jnp.int32, (TILE, SHARD), 1)
            rowstart = jnp.where(rowpos >= n1, n1, jnp.where(rowpos >= n0, n0, 0))

            def fill(t, _):
                kpos = t * TILE + lax.broadcasted_iota(jnp.int32, (TILE, SHARD), 0)
                seen = (kpos <= rowpos) & (kpos >= rowstart)
                bias_s[rs, t] = jnp.where(seen, 0.0, NEG_FILL)
                return 0

            lax.fori_loop(t_lo, t_hi, fill, 0)

        m_s[...] = jnp.full_like(m_s, NEG_FILL)
        l_s[...] = jnp.zeros_like(l_s)
        bm_s[...] = jnp.full_like(bm_s, NEG_FILL)

        def step(t, _):
            parts = []
            for o in range(2):
                j = 2 * t + o
                pos = (j % 8) * 2 + jnp.where(j // 8 != xl, 1, 0)
                parts.append(k_ref[pl.ds(pl.multiple_of(pos * SHARD, SHARD), SHARD), :])
            kt = jnp.concatenate(parts, axis=0)
            bias = bias_s[rs, t]
            for g in range(GROUP):
                s = lax.dot_general(
                    kt,
                    q_ref[:, g * HEAD_DIM : (g + 1) * HEAD_DIM],
                    (((1,), (1,)), ((), ())),
                    preferred_element_type=jnp.float32,
                )
                s = s + bias
                blk = jnp.max(s.reshape(TILE // BLOCK, BLOCK // 8, 8, SHARD), axis=1)
                bm_s[g, pl.ds(t * (TILE // BLOCK), TILE // BLOCK)] = blk
                m_old = m_s[g]
                m_new = jnp.maximum(m_old, jnp.max(blk, axis=0))
                e = jnp.exp2((s.reshape(TILE // 8, 8, SHARD) - m_new[None]) * EXP2_SCALE)
                l_s[g] = l_s[g] * jnp.exp2((m_old - m_new) * EXP2_SCALE) + jnp.sum(e, axis=0)
                m_s[g] = m_new
            return 0

        lax.fori_loop(t_lo, t_hi, step, 0)

        for g in range(GROUP):
            m = m_s[g]
            top = jnp.max(m, axis=0, keepdims=True)
            total = jnp.sum(l_s[g] * jnp.exp2((m - top) * EXP2_SCALE), axis=0, keepdims=True)
            bm = jnp.max(bm_s[g], axis=1)
            p = jnp.exp2((bm - top) * EXP2_SCALE) * (1.0 / total)
            for i in range(2):
                best = jnp.max(p[:, i * BLOCK : (i + 1) * BLOCK], axis=1, keepdims=True)
                col = half * 8 + h * 2 + i
                acc_s[...] += jnp.where(lane == col, best, 0.0)

    @pl.when(h == LOCAL_KV - 1)
    def _():
        raw = acc_s[...]
        norm = raw / jnp.sum(raw, axis=0, keepdims=True)
        out_ref[...] = norm.T[:16, :]


def attention_targets(scalars, q, q_recv, k_all):
    kw = GROUP * HEAD_DIM
    return pl.pallas_call(
        attention_kernel,
        out_shape=jax.ShapeDtypeStruct((16, NUM_BLOCKS), jnp.float32),
        grid_spec=pltpu.PrefetchScalarGridSpec(
            num_scalar_prefetch=1,
            grid=(LOCAL_KV,),
            in_specs=[
                pl.BlockSpec((SHARD, kw), lambda h, sc: (0, sc[2] * LOCAL_KV + h)),
                pl.BlockSpec((SHARD, kw), lambda h, sc: (0, h)),
                pl.BlockSpec((16 * SHARD, HEAD_DIM), lambda h, sc: (0, h)),
            ],
            out_specs=pl.BlockSpec((16, NUM_BLOCKS), lambda h, sc: (0, 0)),
            scratch_shapes=[
                pltpu.VMEM((2, 8, TILE, SHARD), jnp.float32),
                pltpu.VMEM((GROUP, 8, SHARD), jnp.float32),
                pltpu.VMEM((GROUP, 8, SHARD), jnp.float32),
                pltpu.VMEM((GROUP, NUM_BLOCKS, 8, SHARD), jnp.float32),
                pltpu.VMEM((NUM_BLOCKS, 128), jnp.float32),
            ],
        ),
        compiler_params=pltpu.CompilerParams(
            dimension_semantics=("arbitrary",), vmem_limit_bytes=32 * 1024 * 1024
        ),
        cost_estimate=pl.CostEstimate(
            flops=2 * 32 * 128 * 128 * 3072, bytes_accessed=4 << 20, transcendentals=12 << 20
        ),
        name="attention_targets",
    )(scalars, q, q_recv, k_all)


def spread(x, axes, n):
    return lax.all_to_all(
        jnp.broadcast_to(x[None], (n, *x.shape)), axes, split_axis=0, concat_axis=0, tiled=True
    )


def ordered(own, other, index):
    return jnp.where(index == 0, jnp.stack([own, other]), jnp.stack([other, own]))


def shards(queries, keys, doc_ids, gate_query_weight, gate_key_weight):
    xl, y = lax.axis_index("xl"), lax.axis_index("y")
    co, xh = lax.axis_index("co"), lax.axis_index("xh")
    gate_scale = 1.0 / GATE_DIM**0.5
    q, k, doc = queries[0], keys[0], doc_ids[0]
    half_kw, half_qw = k.shape[1] // 2, q.shape[1] // 2

    with jax.named_scope("keys"):
        k_mine = lax.dynamic_slice_in_dim(k, xl * half_kw, half_kw, 1)
        k_other = lax.dynamic_slice_in_dim(k, (1 - xl) * half_kw, half_kw, 1)
        k_recv = lax.ppermute(k_other, "xl", SWAP)
        k_all = lax.all_gather(jnp.concatenate([k_mine, k_recv]), "y", axis=0, tiled=True)
        q_other = lax.dynamic_slice_in_dim(q, (1 - xl) * half_qw, half_qw, 1)
        q_recv = lax.ppermute(q_other, "xl", SWAP)

    with jax.named_scope("pool"):
        pool_q = (
            jnp.sum(q.reshape(2, BLOCK, -1), axis=1, dtype=jnp.float32) / BLOCK
        ).astype(jnp.bfloat16)
        pool_k = jnp.max(k.reshape(2, BLOCK, -1), axis=1)
        mine = jnp.concatenate([pool_q.reshape(2, 16, -1), pool_k.reshape(2, 16, -1)], axis=2)
        pooled = lax.all_to_all(
            mine.transpose(1, 0, 2), CTX_AXES, split_axis=0, concat_axis=0, tiled=True
        ).reshape(NUM_BLOCKS, -1)
    rows_q = gate_query_weight.shape[0]
    rows_k = gate_key_weight.shape[0]
    pooled_q, pooled_k = pooled[:, :rows_q], pooled[:, rows_q:]

    with jax.named_scope("gates"):
        part = jnp.concatenate(
            [
                jnp.dot(pooled_q, gate_query_weight, preferred_element_type=jnp.float32),
                jnp.dot(pooled_k, gate_key_weight, preferred_element_type=jnp.float32),
            ],
            axis=1,
        )
        parts = lax.all_to_all(
            part.reshape(16, 2, -1), CTX_AXES, split_axis=0, concat_axis=0, tiled=True
        )
        gates_mine = jnp.sum(parts, axis=0).astype(jnp.bfloat16)
        gates = spread(gates_mine, CTX_AXES, 16).reshape(NUM_BLOCKS, -1)
        gw = gate_query_weight.shape[1]
        gq = gates[:, :gw].reshape(NUM_BLOCKS, KV_HEADS, GATE_DIM)
        gk = gates[:, gw:].reshape(NUM_BLOCKS, KV_HEADS, GATE_DIM)
        logits = (
            jnp.einsum("ahe,bhe->hab", gq, gk, preferred_element_type=jnp.float32) * gate_scale
        )
        block = jnp.arange(NUM_BLOCKS, dtype=jnp.int32)
        causal = block[None, :] <= block[:, None]
        masked = jnp.where(causal, logits, NEG_FILL)
        peak = jnp.max(masked, axis=-1, keepdims=True)
        weights = jnp.where(causal, jnp.exp(masked - peak), 0.0)
        gate_prob = weights / jnp.sum(weights, axis=-1, keepdims=True)

    with jax.named_scope("pooled_all"):
        hq, hk = rows_q // 2, rows_k // 2

        def half_rows(index):
            return jnp.concatenate(
                [
                    lax.dynamic_slice_in_dim(pooled_q, index * hq, hq, 1),
                    lax.dynamic_slice_in_dim(pooled_k, index * hk, hk, 1),
                ],
                axis=1,
            )

        pair = ordered(half_rows(co), lax.ppermute(half_rows(1 - co), "co", SWAP), co)
        quad = ordered(pair, lax.ppermute(pair, "xh", SWAP), xh)
        pooled_all = lax.all_gather(
            quad.reshape(4 * NUM_BLOCKS, -1), "z", axis=0, tiled=True
        )

    with jax.named_scope("targets"):
        scalars = jnp.stack(
            [
                jnp.sum((doc < 1).astype(jnp.int32)),
                jnp.sum((doc < 2).astype(jnp.int32)),
                xl.astype(jnp.int32),
                y.astype(jnp.int32),
            ]
        )
        mine = attention_targets(scalars, q, q_recv, k_all)
        target = spread(mine, CTX_AXES, 16)
        target = target.reshape(2, 8, 2, LOCAL_KV, 2, NUM_BLOCKS).transpose(0, 3, 2, 1, 4, 5)
        target = target.reshape(KV_HEADS, NUM_BLOCKS, NUM_BLOCKS)

    with jax.named_scope("gate_grads"):
        score_grad = jnp.where(causal, gate_prob - target, 0.0)
        grad_gate_q = (
            jnp.einsum(
                "hab,bhe->hae",
                score_grad,
                gk.astype(jnp.float32),
                precision=lax.Precision.HIGHEST,
            )
            * gate_scale
        ).astype(jnp.bfloat16)
        grad_gate_k = (
            jnp.einsum(
                "hab,ahe->hbe",
                score_grad,
                gq.astype(jnp.float32),
                precision=lax.Precision.HIGHEST,
            )
            * gate_scale
        ).astype(jnp.bfloat16)
        both = jnp.concatenate([grad_gate_q, grad_gate_k], axis=1)
        both = jnp.broadcast_to(both[:, None], (8, 4, 2 * NUM_BLOCKS, GATE_DIM))
        both = lax.all_to_all(
            both.reshape(32, 2 * NUM_BLOCKS, GATE_DIM),
            SEQ_AXES,
            split_axis=0,
            concat_axis=0,
            tiled=True,
        )

    with jax.named_scope("weight_grads"):
        all_q = both[:, :NUM_BLOCKS].reshape(-1, GATE_DIM)
        all_k = both[:, NUM_BLOCKS:].reshape(-1, GATE_DIM)
        piece = jnp.concatenate(
            [
                jnp.dot(pooled_all[:, :hq].T, all_q, preferred_element_type=jnp.float32),
                jnp.dot(pooled_all[:, hq:].T, all_k, preferred_element_type=jnp.float32),
            ]
        ).astype(jnp.bfloat16)
        pieces = spread(piece, "z", 8)
        own = pieces.transpose(1, 0, 2).reshape(hq + hk, -1)
        other = lax.ppermute(own, "co", SWAP)
        out_q = ordered(own[:hq], other[:hq], co).reshape(rows_q, -1)
        out_k = ordered(own[hq:], other[hq:], co).reshape(rows_k, -1)
    return out_q, out_k


def solution(mesh):
    split = Mesh(mesh.devices.reshape(8, 2, 2, 2, 8), (*SEQ_AXES, *CTX_AXES))
    in_specs = (
        P(SEQ_AXES, CTX_AXES, None),
        P(SEQ_AXES, CTX_AXES, None),
        P(SEQ_AXES, None),
        P(CTX_AXES, None),
        P(CTX_AXES, None),
    )
    out_specs = (P(CTX_AXES, None), P(CTX_AXES, None))
    return jax.shard_map(
        shards, mesh=split, in_specs=in_specs, out_specs=out_specs, check_vma=False
    )
```

```python
import functools
import math

import jax
import jax.numpy as jnp
from jax import lax
from jax.experimental import pallas as pl
from jax.experimental.pallas import tpu as pltpu
from jax.sharding import Mesh, PartitionSpec as P

HEADS = 64
KV_HEADS = 8
GROUP = 8
HEAD_DIM = 128
GATE_DIM = 128
BLOCK = 64
SHARD = 128
PANEL = 1024
FOLDED = [0, 4, 2, 6, 1, 5, 3, 7]
LOCAL_KV = 4
NUM_BLOCKS = 32
SEQ_AXES = ("z", "xh", "co")
CTX_AXES = ("xl", "y")
SWAP = [(0, 1), (1, 0)]
NEG_FILL = -1e30
EXP2_SCALE = math.log2(math.e) / math.sqrt(HEAD_DIM)


def attention_kernel(
    sc, q_own, q_recv, k_ref, after, out_ref, bias_s, k_s, q_s, s0, s1, s2, m_s, l_s, bm_s, acc_s
):
    h = pl.program_id(0)
    n0, n1, xl, y = sc[0], sc[1], sc[2], sc[3]
    slots = (s0, s1, s2)
    sub = lax.broadcasted_iota(jnp.int32, (8, SHARD), 0)
    lane = lax.broadcasted_iota(jnp.int32, (NUM_BLOCKS // 2, 128), 1)
    left = lane < BLOCK

    def fold(first, second, span):
        low = (sub & span) == 0
        kept = jnp.where(low, first, second)
        moved = jnp.where(low, second, first)
        if span == 4:
            return jnp.maximum(kept, pltpu.roll(moved, 4, 0))
        turned = jnp.where(low, pltpu.roll(moved, 8 - span, 0), pltpu.roll(moved, span, 0))
        return jnp.maximum(kept, turned)

    panels = ((0, 0), (1, 0), (1, 1))

    @pl.when(h == 0)
    def _():
        acc_s[...] = jnp.zeros_like(acc_s)
        for at, (half, panel) in enumerate(panels):
            rowpos = (half * 8 + y) * SHARD + lax.broadcasted_iota(jnp.int32, (PANEL, SHARD), 1)
            rowstart = jnp.where(rowpos >= n1, n1, jnp.where(rowpos >= n0, n0, 0))
            kpos = panel * PANEL + lax.broadcasted_iota(jnp.int32, (PANEL, SHARD), 0)
            seen = (kpos <= rowpos) & (kpos >= rowstart)
            bias_s[at] = jnp.where(seen, 0.0, NEG_FILL)

    for j in range(16):
        pos = (j % 8) * 2 + jnp.where(xl == j // 8, 0, 1)
        shard = k_ref[pl.ds(pl.multiple_of(pos * SHARD, SHARD), SHARD), :]
        k_s[j * SHARD : (j + 1) * SHARD, :HEAD_DIM] = shard
        k_s[j * SHARD : (j + 1) * SHARD, HEAD_DIM:] = shard
    for g in range(GROUP):
        rows = slice(g * SHARD, (g + 1) * SHARD)
        own = q_own[:, g * HEAD_DIM : (g + 1) * HEAD_DIM].astype(jnp.float32)
        recv = q_recv[:, g * HEAD_DIM : (g + 1) * HEAD_DIM].astype(jnp.float32)
        for half in range(2):
            scaled = jnp.where(xl == half, own, recv) * EXP2_SCALE
            high = scaled.astype(jnp.bfloat16)
            q_s[half, rows, :HEAD_DIM] = high
            q_s[half, rows, HEAD_DIM:] = (scaled - high.astype(jnp.float32)).astype(jnp.bfloat16)

    def scores(item):
        pair, at = divmod(item, 3)
        half, panel = panels[at]
        slots[at][...] = lax.dot_general(
            k_s[panel * PANEL : (panel + 1) * PANEL, :],
            q_s[half, pair * 2 * SHARD : (pair + 1) * 2 * SHARD, :],
            (((1,), (1,)), ((), ())),
            preferred_element_type=jnp.float32,
        )

    def absorb(item):
        pair, at = divmod(item, 3)
        half, panel = panels[at]
        for o in range(2):
            cols = slice(o * SHARD, (o + 1) * SHARD)
            g = pair * 2 + o
            blks = []
            for b in range(PANEL // BLOCK):
                rows = slice(b * BLOCK, (b + 1) * BLOCK)
                s = slots[at][rows, cols] + bias_s[at, rows, :]
                slots[at][rows, cols] = s
                blks.append(jnp.max(s.reshape(BLOCK // 8, 8, SHARD), axis=0))
            top = functools.reduce(jnp.maximum, blks)
            for w in range(PANEL // BLOCK // 8):
                v = [blks[w * 8 + i] for i in FOLDED]
                for span in (4, 2, 1):
                    v = [fold(v[2 * i], v[2 * i + 1], span) for i in range(len(v) // 2)]
                bm_s[half, g, panel * 2 + w] = v[0]
            if panel == 1:
                m_old = m_s[half, g]
                top = jnp.maximum(m_old, top)
            e = jnp.exp2(slots[at][:, cols].reshape(PANEL // 8, 8, SHARD) - top[None])
            total = jnp.sum(e, axis=0)
            if panel == 1:
                total = total + l_s[half, g] * jnp.exp2(m_old - top)
            l_s[half, g] = total
            m_s[half, g] = top

    scores(0)
    for item in range(3 * GROUP // 2):
        if item + 1 < 3 * GROUP // 2:
            scores(item + 1)
        absorb(item)

    for half in range(2):
        for g in range(GROUP):
            m = m_s[half, g]
            top = jnp.max(m, axis=0, keepdims=True)
            total = jnp.sum(l_s[half, g] * jnp.exp2(m - top), axis=0, keepdims=True)
            lse = top + jnp.log2(total)
            for panel in range(half + 1):
                bm = bm_s[half, g, panel * 2 : panel * 2 + 2].reshape(NUM_BLOCKS // 2, SHARD)
                gap = bm - lse
                for i in range(2):
                    held = jnp.where(left if i == 0 else ~left, gap, NEG_FILL)
                    best = jnp.exp2(jnp.max(held, axis=1, keepdims=True))
                    col = half * 8 + h * 2 + i
                    acc_s[panel] += jnp.where(lane == col, best, 0.0)

    @pl.when(h == LOCAL_KV - 1)
    def _():
        raw = acc_s[...].reshape(NUM_BLOCKS, 128)
        norm = raw / jnp.sum(raw, axis=0, keepdims=True)
        out_ref[...] = norm.T[:16, :]


def attention_targets(scalars, q, q_recv, k_all, after):
    kw = GROUP * HEAD_DIM
    return pl.pallas_call(
        attention_kernel,
        out_shape=jax.ShapeDtypeStruct((16, NUM_BLOCKS), jnp.float32),
        grid_spec=pltpu.PrefetchScalarGridSpec(
            num_scalar_prefetch=1,
            grid=(LOCAL_KV,),
            in_specs=[
                pl.BlockSpec((SHARD, kw), lambda h, sc: (0, sc[2] * LOCAL_KV + h)),
                pl.BlockSpec((SHARD, kw), lambda h, sc: (0, h)),
                pl.BlockSpec((16 * SHARD, HEAD_DIM), lambda h, sc: (0, h)),
                pl.BlockSpec(memory_space=pl.ANY),
            ],
            out_specs=pl.BlockSpec((16, NUM_BLOCKS), lambda h, sc: (0, 0)),
            scratch_shapes=[
                pltpu.VMEM((3, PANEL, SHARD), jnp.float32),
                pltpu.VMEM((2 * PANEL, 2 * HEAD_DIM), jnp.bfloat16),
                pltpu.VMEM((2, GROUP * SHARD, 2 * HEAD_DIM), jnp.bfloat16),
                *[pltpu.VMEM((PANEL, 2 * SHARD), jnp.float32) for _ in range(3)],
                pltpu.VMEM((2, GROUP, 8, SHARD), jnp.float32),
                pltpu.VMEM((2, GROUP, 8, SHARD), jnp.float32),
                pltpu.VMEM((2, GROUP, 4, 8, SHARD), jnp.float32),
                pltpu.VMEM((2, NUM_BLOCKS // 2, 128), jnp.float32),
            ],
        ),
        compiler_params=pltpu.CompilerParams(
            dimension_semantics=("arbitrary",), vmem_limit_bytes=32 * 1024 * 1024
        ),
        cost_estimate=pl.CostEstimate(
            flops=2 * 32 * 128 * 128 * 3072, bytes_accessed=4 << 20, transcendentals=12 << 20
        ),
        name="attention_targets",
    )(scalars, q, q_recv, k_all, after)


def assemble_kernel(sc, own, other, out_q, out_k):
    hq, hk = out_q.shape[0] // 2, out_k.shape[0] // 2
    for ref, core in ((own, sc[0]), (other, 1 - sc[0])):
        for z in range(KV_HEADS):
            cols = slice(z * GATE_DIM, (z + 1) * GATE_DIM)
            out_q[pl.ds(pl.multiple_of(core * hq, hq), hq), cols] = ref[z, :hq, :]
            out_k[pl.ds(pl.multiple_of(core * hk, hk), hk), cols] = ref[z, hq:, :]


def assembled(co, own, other, rows_q, rows_k):
    width = KV_HEADS * GATE_DIM
    return pl.pallas_call(
        assemble_kernel,
        out_shape=(
            jax.ShapeDtypeStruct((rows_q, width), jnp.bfloat16),
            jax.ShapeDtypeStruct((rows_k, width), jnp.bfloat16),
        ),
        in_specs=[pl.BlockSpec(memory_space=pltpu.SMEM)]
        + [pl.BlockSpec(memory_space=pltpu.VMEM)] * 2,
        out_specs=(pl.BlockSpec(memory_space=pltpu.VMEM),) * 2,
        compiler_params=pltpu.CompilerParams(vmem_limit_bytes=8 * 1024 * 1024),
        name="assembled",
    )(co.astype(jnp.int32).reshape(1), own, other)


def spread(x, axes, n):
    return lax.all_to_all(
        jnp.broadcast_to(x[None], (n, *x.shape)), axes, split_axis=0, concat_axis=0, tiled=True
    )


def ordered(own, other, index):
    return jnp.where(index == 0, jnp.stack([own, other]), jnp.stack([other, own]))


def shards(queries, keys, doc_ids, gate_query_weight, gate_key_weight):
    xl, y = lax.axis_index("xl"), lax.axis_index("y")
    co, xh = lax.axis_index("co"), lax.axis_index("xh")
    gate_scale = 1.0 / GATE_DIM**0.5
    q, k, doc = queries[0], keys[0], doc_ids[0]
    half_kw, half_qw = k.shape[1] // 2, q.shape[1] // 2

    with jax.named_scope("keys"):
        k_mine = lax.dynamic_slice_in_dim(k, xl * half_kw, half_kw, 1)
        k_other = lax.dynamic_slice_in_dim(k, (1 - xl) * half_kw, half_kw, 1)
        k_recv = lax.ppermute(k_other, "xl", SWAP)
        k_all = lax.all_gather(jnp.concatenate([k_mine, k_recv]), "y", axis=0, tiled=True)
        q_other = lax.dynamic_slice_in_dim(q, (1 - xl) * half_qw, half_qw, 1)
        q_recv = lax.ppermute(q_other, "xl", SWAP)

    with jax.named_scope("pool"):
        pool_q = (
            jnp.sum(q.reshape(2, BLOCK, -1), axis=1, dtype=jnp.float32) / BLOCK
        ).astype(jnp.bfloat16)
        pool_k = jnp.max(k.reshape(2, BLOCK, -1), axis=1)
        mine = jnp.concatenate([pool_q.reshape(2, 16, -1), pool_k.reshape(2, 16, -1)], axis=2)
        pooled = lax.all_to_all(
            mine.transpose(1, 0, 2), CTX_AXES, split_axis=0, concat_axis=0, tiled=True
        ).reshape(NUM_BLOCKS, -1)
    rows_q = gate_query_weight.shape[0]
    rows_k = gate_key_weight.shape[0]
    pooled_q, pooled_k = pooled[:, :rows_q], pooled[:, rows_q:]

    with jax.named_scope("gates"):
        part = jnp.concatenate(
            [
                jnp.dot(pooled_q, gate_query_weight, preferred_element_type=jnp.float32),
                jnp.dot(pooled_k, gate_key_weight, preferred_element_type=jnp.float32),
            ],
            axis=1,
        )
        parts = lax.all_to_all(
            part.reshape(16, 2, -1), CTX_AXES, split_axis=0, concat_axis=0, tiled=True
        )
        gates_mine = jnp.sum(parts, axis=0).astype(jnp.bfloat16)
        gates = spread(gates_mine, CTX_AXES, 16).reshape(NUM_BLOCKS, -1)
        gw = gate_query_weight.shape[1]
        gq = gates[:, :gw].reshape(NUM_BLOCKS, KV_HEADS, GATE_DIM)
        gk = gates[:, gw:].reshape(NUM_BLOCKS, KV_HEADS, GATE_DIM)
        logits = (
            jnp.einsum("ahe,bhe->hab", gq, gk, preferred_element_type=jnp.float32) * gate_scale
        )
        block = jnp.arange(NUM_BLOCKS, dtype=jnp.int32)
        causal = block[None, :] <= block[:, None]
        masked = jnp.where(causal, logits, NEG_FILL)
        peak = jnp.max(masked, axis=-1, keepdims=True)
        weights = jnp.where(causal, jnp.exp(masked - peak), 0.0)
        gate_prob = weights / jnp.sum(weights, axis=-1, keepdims=True)

    with jax.named_scope("pooled_all"):
        pair = ordered(pooled, lax.ppermute(pooled, "co", SWAP), co)
        quad = ordered(pair, lax.ppermute(pair, "xh", SWAP), xh)
        quad = quad.reshape(4 * NUM_BLOCKS, -1)
        pooled_all = lax.all_gather(quad, "z", axis=0, tiled=True)

    with jax.named_scope("targets"):
        scalars = jnp.stack(
            [
                jnp.sum((doc < 1).astype(jnp.int32)),
                jnp.sum((doc < 2).astype(jnp.int32)),
                xl.astype(jnp.int32),
                y.astype(jnp.int32),
            ]
        )
        mine = attention_targets(scalars, q, q_recv, k_all, quad)
        target = spread(mine, CTX_AXES, 16)
        target = target.reshape(2, 8, 2, LOCAL_KV, 2, NUM_BLOCKS).transpose(0, 3, 2, 1, 4, 5)
        target = target.reshape(KV_HEADS, NUM_BLOCKS, NUM_BLOCKS)

    with jax.named_scope("gate_grads"):
        score_grad = jnp.where(causal, gate_prob - target, 0.0)
        grad_gate_q = (
            jnp.einsum(
                "hab,bhe->hae",
                score_grad,
                gk.astype(jnp.float32),
                precision=lax.Precision.HIGHEST,
            )
            * gate_scale
        ).astype(jnp.bfloat16)
        grad_gate_k = (
            jnp.einsum(
                "hab,ahe->hbe",
                score_grad,
                gq.astype(jnp.float32),
                precision=lax.Precision.HIGHEST,
            )
            * gate_scale
        ).astype(jnp.bfloat16)
        both = jnp.concatenate([grad_gate_q, grad_gate_k], axis=1)
        both = jnp.broadcast_to(both[:, None], (8, 4, 2 * NUM_BLOCKS, GATE_DIM))
        both = lax.all_to_all(
            both.reshape(32, 2 * NUM_BLOCKS, GATE_DIM),
            SEQ_AXES,
            split_axis=0,
            concat_axis=0,
            tiled=True,
        )

    with jax.named_scope("weight_grads"):
        all_q = both[:, :NUM_BLOCKS].reshape(-1, GATE_DIM)
        all_k = both[:, NUM_BLOCKS:].reshape(-1, GATE_DIM)
        hq, hk = rows_q // 2, rows_k // 2
        grad_q = jnp.dot(pooled_all[:, :rows_q].T, all_q, preferred_element_type=jnp.float32)
        grad_k = jnp.dot(pooled_all[:, rows_q:].T, all_k, preferred_element_type=jnp.float32)
        piece = jnp.concatenate(
            [
                lax.dynamic_slice_in_dim(grad_q, co * hq, hq, 0),
                lax.dynamic_slice_in_dim(grad_k, co * hk, hk, 0),
            ]
        ).astype(jnp.bfloat16)
        pieces = spread(piece, "z", 8)
        out_q, out_k = assembled(co, pieces, lax.ppermute(pieces, "co", SWAP), rows_q, rows_k)
    return out_q, out_k


def solution(mesh):
    split = Mesh(mesh.devices.reshape(8, 2, 2, 2, 8), (*SEQ_AXES, *CTX_AXES))
    in_specs = (
        P(SEQ_AXES, CTX_AXES, None),
        P(SEQ_AXES, CTX_AXES, None),
        P(SEQ_AXES, None),
        P(CTX_AXES, None),
        P(CTX_AXES, None),
    )
    out_specs = (P(CTX_AXES, None), P(CTX_AXES, None))
    return jax.shard_map(
        shards, mesh=split, in_specs=in_specs, out_specs=out_specs, check_vma=False
    )
```

```python
import math

import jax
import jax.numpy as jnp
from jax import lax
from jax.experimental import pallas as pl
from jax.experimental.pallas import tpu as pltpu
from jax.sharding import Mesh, PartitionSpec as P

HEADS = 64
KV_HEADS = 8
GROUP = 8
HEAD_DIM = 128
GATE_DIM = 128
BLOCK = 64
SHARD = 128
PANEL = 1024
FOLDED = [0, 4, 2, 6, 1, 5, 3, 7]
LOCAL_KV = 4
NUM_BLOCKS = 32
SEQ_AXES = ("z", "xh", "co")
CTX_AXES = ("xl", "y")
SWAP = [(0, 1), (1, 0)]
NEG_FILL = -1e30
EXP2_SCALE = math.log2(math.e) / math.sqrt(HEAD_DIM)


def tree(op, parts):
    while len(parts) > 1:
        parts = [op(a, b) for a, b in zip(parts[::2], parts[1::2], strict=True)]
    return parts[0]


def attention_kernel(
    sc, q_own, q_recv, k_ref, after, out_ref, bias_s, k_s, q_s, s0, s1, s2, m_s, l_s, bm_s, acc_s
):
    h = pl.program_id(0)
    n0, n1, xl, y = sc[0], sc[1], sc[2], sc[3]
    slots = (s0, s1, s2)
    sub = lax.broadcasted_iota(jnp.int32, (8, SHARD), 0)
    lane = lax.broadcasted_iota(jnp.int32, (NUM_BLOCKS // 2, 128), 1)
    left = lane < BLOCK

    def fold(first, second, span):
        low = (sub & span) == 0
        kept = jnp.where(low, first, second)
        moved = jnp.where(low, second, first)
        if span == 4:
            return jnp.maximum(kept, pltpu.roll(moved, 4, 0))
        turned = jnp.where(low, pltpu.roll(moved, 8 - span, 0), pltpu.roll(moved, span, 0))
        return jnp.maximum(kept, turned)

    panels = ((0, 0), (1, 0), (1, 1))

    @pl.when(h == 0)
    def _():
        acc_s[...] = jnp.zeros_like(acc_s)
        for at, (half, panel) in enumerate(panels):
            rowpos = (half * 8 + y) * SHARD + lax.broadcasted_iota(jnp.int32, (PANEL, SHARD), 1)
            rowstart = jnp.where(rowpos >= n1, n1, jnp.where(rowpos >= n0, n0, 0))
            kpos = panel * PANEL + lax.broadcasted_iota(jnp.int32, (PANEL, SHARD), 0)
            seen = (kpos <= rowpos) & (kpos >= rowstart)
            bias_s[at] = jnp.where(seen, 0.0, NEG_FILL)

    for j in range(16):
        pos = (j % 8) * 2 + jnp.where(xl == j // 8, 0, 1)
        shard = k_ref[pl.ds(pl.multiple_of(pos * SHARD, SHARD), SHARD), :]
        k_s[j * SHARD : (j + 1) * SHARD, :HEAD_DIM] = shard
        k_s[j * SHARD : (j + 1) * SHARD, HEAD_DIM:] = shard
    for g in range(GROUP):
        rows = slice(g * SHARD, (g + 1) * SHARD)
        own = q_own[:, g * HEAD_DIM : (g + 1) * HEAD_DIM].astype(jnp.float32)
        recv = q_recv[:, g * HEAD_DIM : (g + 1) * HEAD_DIM].astype(jnp.float32)
        for half in range(2):
            scaled = jnp.where(xl == half, own, recv) * EXP2_SCALE
            high = scaled.astype(jnp.bfloat16)
            q_s[half, rows, :HEAD_DIM] = high
            q_s[half, rows, HEAD_DIM:] = (scaled - high.astype(jnp.float32)).astype(jnp.bfloat16)

    def scores(item):
        pair, at = divmod(item, 3)
        half, panel = panels[at]
        slots[at][...] = lax.dot_general(
            k_s[panel * PANEL : (panel + 1) * PANEL, :],
            q_s[half, pair * 2 * SHARD : (pair + 1) * 2 * SHARD, :],
            (((1,), (1,)), ((), ())),
            preferred_element_type=jnp.float32,
        )

    def absorb(item):
        pair, at = divmod(item, 3)
        half, panel = panels[at]
        for o in range(2):
            cols = slice(o * SHARD, (o + 1) * SHARD)
            g = pair * 2 + o
            blks = []
            for b in range(PANEL // BLOCK):
                rows = slice(b * BLOCK, (b + 1) * BLOCK)
                s = slots[at][rows, cols] + bias_s[at, rows, :]
                slots[at][rows, cols] = s
                blks.append(jnp.max(s.reshape(BLOCK // 8, 8, SHARD), axis=0))
            top = tree(jnp.maximum, blks)
            for w in range(PANEL // BLOCK // 8):
                v = [blks[w * 8 + i] for i in FOLDED]
                for span in (4, 2, 1):
                    v = [fold(v[2 * i], v[2 * i + 1], span) for i in range(len(v) // 2)]
                bm_s[half, g, panel * 2 + w] = v[0]
            if panel == 1:
                m_old = m_s[half, g]
                top = jnp.maximum(m_old, top)
            e = jnp.exp2(slots[at][:, cols].reshape(PANEL // 8, 8, SHARD) - top[None])
            total = tree(jnp.add, [e[b] for b in range(PANEL // 8)])
            if panel == 1:
                total = total + l_s[half, g] * jnp.exp2(m_old - top)
            l_s[half, g] = total
            m_s[half, g] = top

    scores(0)
    for item in range(3 * GROUP // 2):
        if item + 1 < 3 * GROUP // 2:
            scores(item + 1)
        absorb(item)

    for half in range(2):
        for g in range(GROUP):
            m = m_s[half, g]
            top = jnp.max(m, axis=0, keepdims=True)
            total = jnp.sum(l_s[half, g] * jnp.exp2(m - top), axis=0, keepdims=True)
            lse = top + jnp.log2(total)
            for panel in range(half + 1):
                bm = bm_s[half, g, panel * 2 : panel * 2 + 2].reshape(NUM_BLOCKS // 2, SHARD)
                gap = bm - lse
                for i in range(2):
                    held = jnp.where(left if i == 0 else ~left, gap, NEG_FILL)
                    best = jnp.exp2(jnp.max(held, axis=1, keepdims=True))
                    col = half * 8 + h * 2 + i
                    acc_s[panel] += jnp.where(lane == col, best, 0.0)

    @pl.when(h == LOCAL_KV - 1)
    def _():
        raw = acc_s[...].reshape(NUM_BLOCKS, 128)
        norm = raw / jnp.sum(raw, axis=0, keepdims=True)
        mine = norm.T[:16, :]
        for to in range(16):
            out_ref[to * 16 : (to + 1) * 16, :] = mine


def attention_targets(scalars, q, q_recv, k_all, after):
    kw = GROUP * HEAD_DIM
    return pl.pallas_call(
        attention_kernel,
        out_shape=jax.ShapeDtypeStruct((256, NUM_BLOCKS), jnp.float32),
        grid_spec=pltpu.PrefetchScalarGridSpec(
            num_scalar_prefetch=1,
            grid=(LOCAL_KV,),
            in_specs=[
                pl.BlockSpec((SHARD, kw), lambda h, sc: (0, sc[2] * LOCAL_KV + h)),
                pl.BlockSpec((SHARD, kw), lambda h, sc: (0, h)),
                pl.BlockSpec((16 * SHARD, HEAD_DIM), lambda h, sc: (0, h)),
                pl.BlockSpec(memory_space=pl.ANY),
            ],
            out_specs=pl.BlockSpec((256, NUM_BLOCKS), lambda h, sc: (0, 0)),
            scratch_shapes=[
                pltpu.VMEM((3, PANEL, SHARD), jnp.float32),
                pltpu.VMEM((2 * PANEL, 2 * HEAD_DIM), jnp.bfloat16),
                pltpu.VMEM((2, GROUP * SHARD, 2 * HEAD_DIM), jnp.bfloat16),
                *[pltpu.VMEM((PANEL, 2 * SHARD), jnp.float32) for _ in range(3)],
                pltpu.VMEM((2, GROUP, 8, SHARD), jnp.float32),
                pltpu.VMEM((2, GROUP, 8, SHARD), jnp.float32),
                pltpu.VMEM((2, GROUP, 4, 8, SHARD), jnp.float32),
                pltpu.VMEM((2, NUM_BLOCKS // 2, 128), jnp.float32),
            ],
        ),
        compiler_params=pltpu.CompilerParams(
            dimension_semantics=("arbitrary",), vmem_limit_bytes=32 * 1024 * 1024
        ),
        cost_estimate=pl.CostEstimate(
            flops=2 * 32 * 128 * 128 * 3072, bytes_accessed=4 << 20, transcendentals=12 << 20
        ),
        name="attention_targets",
    )(scalars, q, q_recv, k_all, after)


def gate_grads_kernel(target, prob, gq, gk, out_ref):
    left = lax.broadcasted_iota(jnp.int32, (NUM_BLOCKS, GATE_DIM), 1) < GATE_DIM // 2
    row = lax.broadcasted_iota(jnp.int32, (NUM_BLOCKS, NUM_BLOCKS), 0)
    causal = lax.broadcasted_iota(jnp.int32, (NUM_BLOCKS, NUM_BLOCKS), 1) <= row
    scale = 1.0 / GATE_DIM**0.5

    def product(grad, other):
        high = grad.astype(jnp.bfloat16)
        low = (grad - high.astype(jnp.float32)).astype(jnp.bfloat16)
        total = jnp.dot(high, other, preferred_element_type=jnp.float32)
        total = total + jnp.dot(low, other, preferred_element_type=jnp.float32)
        return (total * scale).astype(jnp.bfloat16).astype(jnp.float32)

    for head in range(KV_HEADS):
        cols = slice(head * GATE_DIM, (head + 1) * GATE_DIM)
        x, h = divmod(head, LOCAL_KV)
        rows = [(x * 8 + y) * 16 + half * 8 + h * 2 for half in range(2) for y in range(8)]
        mine = jnp.concatenate([target[r : r + 2, :] for r in rows], axis=0)
        grad = jnp.where(causal, prob[head] - mine, 0.0)
        of_q = product(grad, gk[:, cols])
        of_k = product(grad.T, gq[:, cols])
        half = GATE_DIM // 2
        first = jnp.where(left, of_q, pltpu.roll(of_k, half, 1)).astype(jnp.bfloat16)
        second = jnp.where(left, pltpu.roll(of_q, half, 1), of_k).astype(jnp.bfloat16)
        for to in range(4):
            at = (head * 4 + to) * NUM_BLOCKS
            out_ref[at : at + NUM_BLOCKS, :] = first if to % 2 == 0 else second


def weight_grads_kernel(pooled, grads, out_ref):
    depth = 4 * NUM_BLOCKS
    rows = pooled.shape[0] // 8
    total = jnp.zeros((rows, GATE_DIM), jnp.float32)
    for z in range(8):
        total = total + jnp.dot(
            pooled[z * rows : (z + 1) * rows, :],
            grads[z * depth : (z + 1) * depth, :],
            preferred_element_type=jnp.float32,
        )
    rows_k = rows // 9
    hq, hk = rows_k * 4, rows_k // 2
    of_q, of_k = total[: 2 * hq], total[2 * hq :]
    left = lax.broadcasted_iota(jnp.int32, (hq, GATE_DIM), 1) < GATE_DIM // 2
    half = GATE_DIM // 2
    top = jnp.where(left, of_q[:hq], pltpu.roll(of_q[hq:], half, 1)).astype(jnp.bfloat16)
    low = jnp.where(left[:hk], pltpu.roll(of_k[:hk], half, 1), of_k[hk:]).astype(jnp.bfloat16)
    for z in range(8):
        out_ref[z, :hq, :] = top
        out_ref[z, hq:, :] = low


def assemble_kernel(sc, own, other, out_q, out_k):
    hq, hk = out_q.shape[0] // 2, out_k.shape[0] // 2
    half = GATE_DIM // 2
    left = lax.broadcasted_iota(jnp.int32, (hq + hk, GATE_DIM), 1) < half
    first = sc[0] == 0
    for z in range(KV_HEADS):
        cols = slice(z * GATE_DIM, (z + 1) * GATE_DIM)
        mine, theirs = own[z].astype(jnp.float32), other[z].astype(jnp.float32)
        core0 = jnp.where(first, mine, theirs)
        core1 = jnp.where(first, theirs, mine)
        upper = jnp.where(left, core0, pltpu.roll(core1, half, 1)).astype(jnp.bfloat16)
        lower = jnp.where(left, pltpu.roll(core0, half, 1), core1).astype(jnp.bfloat16)
        out_q[:hq, cols] = upper[:hq]
        out_q[hq:, cols] = lower[:hq]
        out_k[:hk, cols] = upper[hq:]
        out_k[hk:, cols] = lower[hq:]


def in_vmem(kernel, out_shape, name, mib, *args):
    spec = pl.BlockSpec(memory_space=pltpu.VMEM)
    return pl.pallas_call(
        kernel,
        out_shape=out_shape,
        in_specs=[spec] * len(args),
        out_specs=spec,
        compiler_params=pltpu.CompilerParams(vmem_limit_bytes=mib * 1024 * 1024),
        name=name,
    )(*args)


def assembled(co, own, other, rows_q, rows_k):
    width = KV_HEADS * GATE_DIM
    return pl.pallas_call(
        assemble_kernel,
        out_shape=(
            jax.ShapeDtypeStruct((rows_q, width), jnp.bfloat16),
            jax.ShapeDtypeStruct((rows_k, width), jnp.bfloat16),
        ),
        in_specs=[pl.BlockSpec(memory_space=pltpu.SMEM)]
        + [pl.BlockSpec(memory_space=pltpu.VMEM)] * 2,
        out_specs=(pl.BlockSpec(memory_space=pltpu.VMEM),) * 2,
        compiler_params=pltpu.CompilerParams(vmem_limit_bytes=8 * 1024 * 1024),
        name="assembled",
    )(co.astype(jnp.int32).reshape(1), own, other)


def spread(x, axes, n):
    return lax.all_to_all(
        jnp.broadcast_to(x[None], (n, *x.shape)), axes, split_axis=0, concat_axis=0, tiled=True
    )


def ordered(own, other, index):
    return jnp.where(index == 0, jnp.stack([own, other]), jnp.stack([other, own]))


def shards(queries, keys, doc_ids, gate_query_weight, gate_key_weight):
    xl, y = lax.axis_index("xl"), lax.axis_index("y")
    co, xh = lax.axis_index("co"), lax.axis_index("xh")
    gate_scale = 1.0 / GATE_DIM**0.5
    q, k, doc = queries[0], keys[0], doc_ids[0]
    half_kw, half_qw = k.shape[1] // 2, q.shape[1] // 2

    with jax.named_scope("keys"):
        k_mine = lax.dynamic_slice_in_dim(k, xl * half_kw, half_kw, 1)
        k_other = lax.dynamic_slice_in_dim(k, (1 - xl) * half_kw, half_kw, 1)
        k_recv = lax.ppermute(k_other, "xl", SWAP)
        k_all = lax.all_gather(jnp.concatenate([k_mine, k_recv]), "y", axis=0, tiled=True)
        q_other = lax.dynamic_slice_in_dim(q, (1 - xl) * half_qw, half_qw, 1)
        q_recv = lax.ppermute(q_other, "xl", SWAP)

    with jax.named_scope("pool"):
        pool_q = (
            jnp.sum(q.reshape(2, BLOCK, -1), axis=1, dtype=jnp.float32) / BLOCK
        ).astype(jnp.bfloat16)
        pool_k = jnp.max(k.reshape(2, BLOCK, -1), axis=1)
        mine = jnp.concatenate([pool_q.reshape(2, 16, -1), pool_k.reshape(2, 16, -1)], axis=2)
        pooled = lax.all_to_all(
            mine.transpose(1, 0, 2), CTX_AXES, split_axis=0, concat_axis=0, tiled=True
        ).reshape(NUM_BLOCKS, -1)
    rows_q = gate_query_weight.shape[0]
    rows_k = gate_key_weight.shape[0]
    pooled_q, pooled_k = pooled[:, :rows_q], pooled[:, rows_q:]

    with jax.named_scope("gates"):
        part = jnp.concatenate(
            [
                jnp.dot(pooled_q, gate_query_weight, preferred_element_type=jnp.float32),
                jnp.dot(pooled_k, gate_key_weight, preferred_element_type=jnp.float32),
            ],
            axis=1,
        )
        parts = lax.all_to_all(
            part.reshape(16, 2, -1), CTX_AXES, split_axis=0, concat_axis=0, tiled=True
        )
        gates_mine = jnp.sum(parts, axis=0).astype(jnp.bfloat16)
        gates = spread(gates_mine, CTX_AXES, 16).reshape(NUM_BLOCKS, -1)
        gw = gate_query_weight.shape[1]
        gq = gates[:, :gw].reshape(NUM_BLOCKS, KV_HEADS, GATE_DIM)
        gk = gates[:, gw:].reshape(NUM_BLOCKS, KV_HEADS, GATE_DIM)
        logits = (
            jnp.einsum("ahe,bhe->hab", gq, gk, preferred_element_type=jnp.float32) * gate_scale
        )
        block = jnp.arange(NUM_BLOCKS, dtype=jnp.int32)
        causal = block[None, :] <= block[:, None]
        masked = jnp.where(causal, logits, NEG_FILL)
        peak = jnp.max(masked, axis=-1, keepdims=True)
        weights = jnp.where(causal, jnp.exp(masked - peak), 0.0)
        gate_prob = weights / jnp.sum(weights, axis=-1, keepdims=True)

    with jax.named_scope("pooled_all"):
        pair = ordered(pooled, lax.ppermute(pooled, "co", SWAP), co)
        quad = ordered(pair, lax.ppermute(pair, "xh", SWAP), xh)
        quad = quad.reshape(4 * NUM_BLOCKS, -1).T
        pooled_all = lax.all_gather(quad, "z", axis=0, tiled=True)

    with jax.named_scope("targets"):
        scalars = jnp.stack(
            [
                jnp.sum((doc < 1).astype(jnp.int32)),
                jnp.sum((doc < 2).astype(jnp.int32)),
                xl.astype(jnp.int32),
                y.astype(jnp.int32),
            ]
        )
        mine = attention_targets(scalars, q, q_recv, k_all, quad)
        target = lax.all_to_all(mine, CTX_AXES, split_axis=0, concat_axis=0, tiled=True)

    with jax.named_scope("gate_grads"):
        grads = in_vmem(
            gate_grads_kernel,
            jax.ShapeDtypeStruct((32 * NUM_BLOCKS, GATE_DIM), jnp.bfloat16),
            "gate_grads",
            16,
            target,
            gate_prob,
            gates[:, :gw],
            gates[:, gw:],
        )
        grads = lax.all_to_all(grads, SEQ_AXES, split_axis=0, concat_axis=0, tiled=True)

    with jax.named_scope("weight_grads"):
        pieces = in_vmem(
            weight_grads_kernel,
            jax.ShapeDtypeStruct((8, (rows_q + rows_k) // 2, GATE_DIM), jnp.bfloat16),
            "weight_grads",
            16,
            pooled_all,
            grads,
        )
        pieces = lax.all_to_all(pieces, "z", split_axis=0, concat_axis=0, tiled=True)
        out_q, out_k = assembled(co, pieces, lax.ppermute(pieces, "co", SWAP), rows_q, rows_k)
    return out_q, out_k


def solution(mesh):
    split = Mesh(mesh.devices.reshape(8, 2, 2, 2, 8), (*SEQ_AXES, *CTX_AXES))
    in_specs = (
        P(SEQ_AXES, CTX_AXES, None),
        P(SEQ_AXES, CTX_AXES, None),
        P(SEQ_AXES, None),
        P(CTX_AXES, None),
        P(CTX_AXES, None),
    )
    out_specs = (P(CTX_AXES, None), P(CTX_AXES, None))
    return jax.shard_map(
        shards, mesh=split, in_specs=in_specs, out_specs=out_specs, check_vma=False
    )
```

```python
import math

import jax
import jax.numpy as jnp
from jax import lax
from jax.experimental import pallas as pl
from jax.experimental.pallas import tpu as pltpu
from jax.sharding import Mesh, PartitionSpec as P

HEADS = 64
KV_HEADS = 8
GROUP = 8
HEAD_DIM = 128
GATE_DIM = 128
BLOCK = 64
SHARD = 128
PANEL = 1024
FOLDED = [0, 4, 2, 6, 1, 5, 3, 7]
LOCAL_KV = 4
NUM_BLOCKS = 32
SEQ_AXES = ("z", "xh", "co")
CTX_AXES = ("xl", "y")
SWAP = [(0, 1), (1, 0)]
NEG_FILL = -1e30
EXP2_SCALE = math.log2(math.e) / math.sqrt(HEAD_DIM)


def tree(op, parts):
    while len(parts) > 1:
        parts = [op(a, b) for a, b in zip(parts[::2], parts[1::2], strict=True)]
    return parts[0]


def attention_kernel(
    sc, q_own, q_recv, k_ref, gates, after, out_ref, bias_s, k_s, q_s, s0, s1, s2, m_s, l_s, bm_s, acc_s
):
    h = pl.program_id(0)
    n0, n1, xl, y = sc[0], sc[1], sc[2], sc[3]
    slots = (s0, s1, s2)
    sub = lax.broadcasted_iota(jnp.int32, (8, SHARD), 0)
    lane = lax.broadcasted_iota(jnp.int32, (NUM_BLOCKS // 2, 128), 1)
    left = lane < BLOCK

    def fold(first, second, span):
        low = (sub & span) == 0
        kept = jnp.where(low, first, second)
        moved = jnp.where(low, second, first)
        if span == 4:
            return jnp.maximum(kept, pltpu.roll(moved, 4, 0))
        turned = jnp.where(low, pltpu.roll(moved, 8 - span, 0), pltpu.roll(moved, span, 0))
        return jnp.maximum(kept, turned)

    panels = ((0, 0), (1, 0), (1, 1))

    @pl.when(h == 0)
    def _():
        acc_s[...] = jnp.zeros_like(acc_s)
        for at, (half, panel) in enumerate(panels):
            rowpos = (half * 8 + y) * SHARD + lax.broadcasted_iota(jnp.int32, (PANEL, SHARD), 1)
            rowstart = jnp.where(rowpos >= n1, n1, jnp.where(rowpos >= n0, n0, 0))
            kpos = panel * PANEL + lax.broadcasted_iota(jnp.int32, (PANEL, SHARD), 0)
            seen = (kpos <= rowpos) & (kpos >= rowstart)
            bias_s[at] = jnp.where(seen, 0.0, NEG_FILL)

    for j in range(16):
        pos = (j % 8) * 2 + jnp.where(xl == j // 8, 0, 1)
        shard = k_ref[pl.ds(pl.multiple_of(pos * SHARD, SHARD), SHARD), :]
        k_s[j * SHARD : (j + 1) * SHARD, :HEAD_DIM] = shard
        k_s[j * SHARD : (j + 1) * SHARD, HEAD_DIM:] = shard
    for g in range(GROUP):
        rows = slice(g * SHARD, (g + 1) * SHARD)
        own = q_own[:, g * HEAD_DIM : (g + 1) * HEAD_DIM].astype(jnp.float32)
        recv = q_recv[:, g * HEAD_DIM : (g + 1) * HEAD_DIM].astype(jnp.float32)
        for half in range(2):
            scaled = jnp.where(xl == half, own, recv) * EXP2_SCALE
            high = scaled.astype(jnp.bfloat16)
            q_s[half, rows, :HEAD_DIM] = high
            q_s[half, rows, HEAD_DIM:] = (scaled - high.astype(jnp.float32)).astype(jnp.bfloat16)

    def scores(item):
        pair, at = divmod(item, 3)
        half, panel = panels[at]
        slots[at][...] = lax.dot_general(
            k_s[panel * PANEL : (panel + 1) * PANEL, :],
            q_s[half, pair * 2 * SHARD : (pair + 1) * 2 * SHARD, :],
            (((1,), (1,)), ((), ())),
            preferred_element_type=jnp.float32,
        )

    def absorb(item):
        pair, at = divmod(item, 3)
        half, panel = panels[at]
        for o in range(2):
            cols = slice(o * SHARD, (o + 1) * SHARD)
            g = pair * 2 + o
            blks = []
            for b in range(PANEL // BLOCK):
                rows = slice(b * BLOCK, (b + 1) * BLOCK)
                s = slots[at][rows, cols] + bias_s[at, rows, :]
                slots[at][rows, cols] = s
                blks.append(jnp.max(s.reshape(BLOCK // 8, 8, SHARD), axis=0))
            top = tree(jnp.maximum, blks)
            for w in range(PANEL // BLOCK // 8):
                v = [blks[w * 8 + i] for i in FOLDED]
                for span in (4, 2, 1):
                    v = [fold(v[2 * i], v[2 * i + 1], span) for i in range(len(v) // 2)]
                bm_s[half, g, panel * 2 + w] = v[0]
            if panel == 1:
                m_old = m_s[half, g]
                top = jnp.maximum(m_old, top)
            e = jnp.exp2(slots[at][:, cols].reshape(PANEL // 8, 8, SHARD) - top[None])
            total = tree(jnp.add, [e[b] for b in range(PANEL // 8)])
            if panel == 1:
                total = total + l_s[half, g] * jnp.exp2(m_old - top)
            l_s[half, g] = total
            m_s[half, g] = top

    scores(0)
    for item in range(3 * GROUP // 2):
        if item + 1 < 3 * GROUP // 2:
            scores(item + 1)
        absorb(item)

    for half in range(2):
        for g in range(GROUP):
            m = m_s[half, g]
            top = jnp.max(m, axis=0, keepdims=True)
            total = jnp.sum(l_s[half, g] * jnp.exp2(m - top), axis=0, keepdims=True)
            lse = top + jnp.log2(total)
            for panel in range(half + 1):
                bm = bm_s[half, g, panel * 2 : panel * 2 + 2].reshape(NUM_BLOCKS // 2, SHARD)
                gap = bm - lse
                for i in range(2):
                    held = jnp.where(left if i == 0 else ~left, gap, NEG_FILL)
                    best = jnp.exp2(jnp.max(held, axis=1, keepdims=True))
                    col = half * 8 + h * 2 + i
                    acc_s[panel] += jnp.where(lane == col, best, 0.0)

    @pl.when(h == LOCAL_KV - 1)
    def _():
        raw = acc_s[...].reshape(NUM_BLOCKS, 128)
        norm = raw / jnp.sum(raw, axis=0, keepdims=True)
        high = norm.astype(jnp.bfloat16).astype(jnp.float32)
        parts = jnp.concatenate([high, norm - high, jnp.zeros((64, 128), jnp.float32)], axis=0)
        mine = parts.T[:16, :].astype(jnp.bfloat16)
        for to in range(16):
            out_ref[to * 48 : to * 48 + 32, :] = gates[...]
            out_ref[to * 48 + 32 : to * 48 + 48, :] = mine


def attention_targets(scalars, q, q_recv, k_all, gates, after):
    kw = GROUP * HEAD_DIM
    return pl.pallas_call(
        attention_kernel,
        out_shape=jax.ShapeDtypeStruct((16 * 48, 128), jnp.bfloat16),
        grid_spec=pltpu.PrefetchScalarGridSpec(
            num_scalar_prefetch=1,
            grid=(LOCAL_KV,),
            in_specs=[
                pl.BlockSpec((SHARD, kw), lambda h, sc: (0, sc[2] * LOCAL_KV + h)),
                pl.BlockSpec((SHARD, kw), lambda h, sc: (0, h)),
                pl.BlockSpec((16 * SHARD, HEAD_DIM), lambda h, sc: (0, h)),
                pl.BlockSpec((32, 128), lambda h, sc: (0, 0)),
                pl.BlockSpec(memory_space=pl.ANY),
            ],
            out_specs=pl.BlockSpec((16 * 48, 128), lambda h, sc: (0, 0)),
            scratch_shapes=[
                pltpu.VMEM((3, PANEL, SHARD), jnp.float32),
                pltpu.VMEM((2 * PANEL, 2 * HEAD_DIM), jnp.bfloat16),
                pltpu.VMEM((2, GROUP * SHARD, 2 * HEAD_DIM), jnp.bfloat16),
                *[pltpu.VMEM((PANEL, 2 * SHARD), jnp.float32) for _ in range(3)],
                pltpu.VMEM((2, GROUP, 8, SHARD), jnp.float32),
                pltpu.VMEM((2, GROUP, 8, SHARD), jnp.float32),
                pltpu.VMEM((2, GROUP, 4, 8, SHARD), jnp.float32),
                pltpu.VMEM((2, NUM_BLOCKS // 2, 128), jnp.float32),
            ],
        ),
        compiler_params=pltpu.CompilerParams(
            dimension_semantics=("arbitrary",), vmem_limit_bytes=56 * 1024 * 1024
        ),
        cost_estimate=pl.CostEstimate(
            flops=2 * 32 * 128 * 128 * 3072, bytes_accessed=4 << 20, transcendentals=12 << 20
        ),
        name="attention_targets",
    )(scalars, q, q_recv, k_all, gates, after)


def gate_grads_kernel(target, gates, out_ref):
    left = lax.broadcasted_iota(jnp.int32, (NUM_BLOCKS, GATE_DIM), 1) < GATE_DIM // 2
    row = lax.broadcasted_iota(jnp.int32, (NUM_BLOCKS, NUM_BLOCKS), 0)
    causal = lax.broadcasted_iota(jnp.int32, (NUM_BLOCKS, NUM_BLOCKS), 1) <= row
    scale = 1.0 / GATE_DIM**0.5

    def product(grad, other):
        high = grad.astype(jnp.bfloat16)
        low = (grad - high.astype(jnp.float32)).astype(jnp.bfloat16)
        total = jnp.dot(high, other, preferred_element_type=jnp.float32)
        total = total + jnp.dot(low, other, preferred_element_type=jnp.float32)
        return (total * scale).astype(jnp.bfloat16).astype(jnp.float32)

    for head in range(KV_HEADS):
        gq, gk = gates[head], gates[KV_HEADS + head]
        logits = lax.dot_general(
            gq, gk, (((1,), (1,)), ((), ())), preferred_element_type=jnp.float32
        )
        logits = jnp.where(causal, logits * scale, NEG_FILL)
        weights = jnp.exp(logits - jnp.max(logits, axis=1, keepdims=True))
        weights = jnp.where(causal, weights, 0.0)
        prob = weights / jnp.sum(weights, axis=1, keepdims=True)
        grad = jnp.where(causal, prob - target[head], 0.0)
        of_q = product(grad, gk)
        of_k = product(grad.T, gq)
        half = GATE_DIM // 2
        first = jnp.where(left, of_q, pltpu.roll(of_k, half, 1)).astype(jnp.bfloat16)
        second = jnp.where(left, pltpu.roll(of_q, half, 1), of_k).astype(jnp.bfloat16)
        for to in range(4):
            at = (head * 4 + to) * NUM_BLOCKS
            out_ref[at : at + NUM_BLOCKS, :] = first if to % 2 == 0 else second


def weight_grads_kernel(pooled, grads, out_ref):
    depth = 4 * NUM_BLOCKS
    rows = pooled.shape[0] // 8
    total = jnp.zeros((rows, GATE_DIM), jnp.float32)
    for z in range(8):
        total = total + jnp.dot(
            pooled[z * rows : (z + 1) * rows, :],
            grads[z * depth : (z + 1) * depth, :],
            preferred_element_type=jnp.float32,
        )
    rows_k = rows // 9
    hq, hk = rows_k * 4, rows_k // 2
    of_q, of_k = total[: 2 * hq], total[2 * hq :]
    left = lax.broadcasted_iota(jnp.int32, (hq, GATE_DIM), 1) < GATE_DIM // 2
    half = GATE_DIM // 2
    top = jnp.where(left, of_q[:hq], pltpu.roll(of_q[hq:], half, 1)).astype(jnp.bfloat16)
    low = jnp.where(left[:hk], pltpu.roll(of_k[:hk], half, 1), of_k[hk:]).astype(jnp.bfloat16)
    for z in range(8):
        out_ref[z, :hq, :] = top
        out_ref[z, hq:, :] = low


def assemble_kernel(sc, own, other, out_q, out_k):
    hq, hk = out_q.shape[0] // 2, out_k.shape[0] // 2
    half = GATE_DIM // 2
    left = lax.broadcasted_iota(jnp.int32, (hq + hk, GATE_DIM), 1) < half
    first = sc[0] == 0
    for z in range(KV_HEADS):
        cols = slice(z * GATE_DIM, (z + 1) * GATE_DIM)
        mine, theirs = own[z].astype(jnp.float32), other[z].astype(jnp.float32)
        core0 = jnp.where(first, mine, theirs)
        core1 = jnp.where(first, theirs, mine)
        upper = jnp.where(left, core0, pltpu.roll(core1, half, 1)).astype(jnp.bfloat16)
        lower = jnp.where(left, pltpu.roll(core0, half, 1), core1).astype(jnp.bfloat16)
        out_q[:hq, cols] = upper[:hq]
        out_q[hq:, cols] = lower[:hq]
        out_k[:hk, cols] = upper[hq:]
        out_k[hk:, cols] = lower[hq:]


def in_vmem(kernel, out_shape, name, mib, *args):
    spec = pl.BlockSpec(memory_space=pltpu.VMEM)
    return pl.pallas_call(
        kernel,
        out_shape=out_shape,
        in_specs=[spec] * len(args),
        out_specs=spec,
        compiler_params=pltpu.CompilerParams(vmem_limit_bytes=mib * 1024 * 1024),
        name=name,
    )(*args)


def assembled(co, own, other, rows_q, rows_k):
    width = KV_HEADS * GATE_DIM
    return pl.pallas_call(
        assemble_kernel,
        out_shape=(
            jax.ShapeDtypeStruct((rows_q, width), jnp.bfloat16),
            jax.ShapeDtypeStruct((rows_k, width), jnp.bfloat16),
        ),
        in_specs=[pl.BlockSpec(memory_space=pltpu.SMEM)]
        + [pl.BlockSpec(memory_space=pltpu.VMEM)] * 2,
        out_specs=(pl.BlockSpec(memory_space=pltpu.VMEM),) * 2,
        compiler_params=pltpu.CompilerParams(vmem_limit_bytes=8 * 1024 * 1024),
        name="assembled",
    )(co.astype(jnp.int32).reshape(1), own, other)


def ordered(own, other, index):
    return jnp.where(index == 0, jnp.stack([own, other]), jnp.stack([other, own]))


def shards(queries, keys, doc_ids, gate_query_weight, gate_key_weight):
    xl, y = lax.axis_index("xl"), lax.axis_index("y")
    co, xh = lax.axis_index("co"), lax.axis_index("xh")
    q, k, doc = queries[0], keys[0], doc_ids[0]
    half_kw, half_qw = k.shape[1] // 2, q.shape[1] // 2

    with jax.named_scope("keys"):
        k_mine = lax.dynamic_slice_in_dim(k, xl * half_kw, half_kw, 1)
        k_other = lax.dynamic_slice_in_dim(k, (1 - xl) * half_kw, half_kw, 1)
        k_recv = lax.ppermute(k_other, "xl", SWAP)
        k_all = lax.all_gather(jnp.concatenate([k_mine, k_recv]), "y", axis=0, tiled=True)
        q_other = lax.dynamic_slice_in_dim(q, (1 - xl) * half_qw, half_qw, 1)
        q_recv = lax.ppermute(q_other, "xl", SWAP)

    with jax.named_scope("pool"):
        pool_q = (
            jnp.sum(q.reshape(2, BLOCK, -1), axis=1, dtype=jnp.float32) / BLOCK
        ).astype(jnp.bfloat16)
        pool_k = jnp.max(k.reshape(2, BLOCK, -1), axis=1)
        mine = jnp.concatenate([pool_q.reshape(2, 16, -1), pool_k.reshape(2, 16, -1)], axis=2)
        pooled = lax.all_to_all(
            mine.transpose(1, 0, 2), CTX_AXES, split_axis=0, concat_axis=0, tiled=True
        ).reshape(NUM_BLOCKS, -1)
    rows_q = gate_query_weight.shape[0]
    rows_k = gate_key_weight.shape[0]
    pooled_q, pooled_k = pooled[:, :rows_q], pooled[:, rows_q:]

    with jax.named_scope("gates"):
        part = jnp.concatenate(
            [
                jnp.dot(pooled_q, gate_query_weight, preferred_element_type=jnp.float32),
                jnp.dot(pooled_k, gate_key_weight, preferred_element_type=jnp.float32),
            ],
            axis=1,
        )
        parts = lax.all_to_all(
            part.reshape(16, 2, -1), CTX_AXES, split_axis=0, concat_axis=0, tiled=True
        )
        gates_mine = jnp.sum(parts, axis=0).astype(jnp.bfloat16)
        gates_mine = gates_mine.reshape(2, 16, GATE_DIM).transpose(1, 0, 2).reshape(32, GATE_DIM)

    with jax.named_scope("pooled_all"):
        pair = ordered(pooled, lax.ppermute(pooled, "co", SWAP), co)
        quad = ordered(pair, lax.ppermute(pair, "xh", SWAP), xh)
        quad = quad.reshape(4 * NUM_BLOCKS, -1).T
        pooled_all = lax.all_gather(quad, "z", axis=0, tiled=True)

    with jax.named_scope("targets"):
        scalars = jnp.stack(
            [
                jnp.sum((doc < 1).astype(jnp.int32)),
                jnp.sum((doc < 2).astype(jnp.int32)),
                xl.astype(jnp.int32),
                y.astype(jnp.int32),
            ]
        )
        mine = attention_targets(scalars, q, q_recv, k_all, gates_mine, quad)
        both = lax.all_to_all(mine, CTX_AXES, split_axis=0, concat_axis=0, tiled=True)
        both = both.reshape(16, 48, 128)

    with jax.named_scope("gate_grads"):
        gates = both[:, :32].reshape(16, 16, 2, GATE_DIM).transpose(1, 0, 2, 3)
        target = both[:, 32:, :NUM_BLOCKS].astype(jnp.float32)
        target = target + both[:, 32:, NUM_BLOCKS : 2 * NUM_BLOCKS].astype(jnp.float32)
        target = target.reshape(2, 8, 2, LOCAL_KV, 2, NUM_BLOCKS).transpose(0, 3, 2, 1, 4, 5)
        grads = in_vmem(
            gate_grads_kernel,
            jax.ShapeDtypeStruct((32 * NUM_BLOCKS, GATE_DIM), jnp.bfloat16),
            "gate_grads",
            16,
            target.reshape(KV_HEADS, NUM_BLOCKS, NUM_BLOCKS),
            gates.reshape(16, NUM_BLOCKS, GATE_DIM),
        )
        grads = lax.all_to_all(grads, SEQ_AXES, split_axis=0, concat_axis=0, tiled=True)

    with jax.named_scope("weight_grads"):
        pieces = in_vmem(
            weight_grads_kernel,
            jax.ShapeDtypeStruct((8, (rows_q + rows_k) // 2, GATE_DIM), jnp.bfloat16),
            "weight_grads",
            16,
            pooled_all,
            grads,
        )
        pieces = lax.all_to_all(pieces, "z", split_axis=0, concat_axis=0, tiled=True)
        out_q, out_k = assembled(co, pieces, lax.ppermute(pieces, "co", SWAP), rows_q, rows_k)
    return out_q, out_k


def solution(mesh):
    split = Mesh(mesh.devices.reshape(8, 2, 2, 2, 8), (*SEQ_AXES, *CTX_AXES))
    in_specs = (
        P(SEQ_AXES, CTX_AXES, None),
        P(SEQ_AXES, CTX_AXES, None),
        P(SEQ_AXES, None),
        P(CTX_AXES, None),
        P(CTX_AXES, None),
    )
    out_specs = (P(CTX_AXES, None), P(CTX_AXES, None))
    return jax.shard_map(
        shards, mesh=split, in_specs=in_specs, out_specs=out_specs, check_vma=False
    )
```

```python
import functools
import math

import jax
import jax.numpy as jnp
from jax import lax
from jax.experimental import pallas as pl
from jax.experimental.pallas import tpu as pltpu
from jax.sharding import Mesh, PartitionSpec as P

HEADS = 64
KV_HEADS = 8
GROUP = 8
HEAD_DIM = 128
GATE_DIM = 128
BLOCK = 64
SHARD = 128
PANEL = 1024
FOLDED = [0, 4, 2, 6, 1, 5, 3, 7]
LOCAL_KV = 4
PART_KV = 2
NUM_BLOCKS = 32
SEQ_AXES = ("z", "xh", "co")
CTX_AXES = ("xl", "y")
SWAP = [(0, 1), (1, 0)]
NEG_FILL = -1e30
EXP2_SCALE = math.log2(math.e) / math.sqrt(HEAD_DIM)


def tree(op, parts):
    while len(parts) > 1:
        parts = [op(a, b) for a, b in zip(parts[::2], parts[1::2], strict=True)]
    return parts[0]


def attention_kernel(part, sc, q_own, q_recv, k_ref, *refs):
    if part == 0:
        out_ref, *scratch = refs
    else:
        gates, before, _, out_ref, *scratch = refs
    bias_s, k_s, q_s, s0, s1, s2, m_s, l_s, bm_s, acc_s = scratch
    h = pl.program_id(0)
    n0, n1, xl, y = sc[0], sc[1], sc[2], sc[3]
    slots = (s0, s1, s2)
    sub = lax.broadcasted_iota(jnp.int32, (8, SHARD), 0)
    lane = lax.broadcasted_iota(jnp.int32, (NUM_BLOCKS // 2, 128), 1)
    left = lane < BLOCK

    def fold(first, second, span):
        low = (sub & span) == 0
        kept = jnp.where(low, first, second)
        moved = jnp.where(low, second, first)
        if span == 4:
            return jnp.maximum(kept, pltpu.roll(moved, 4, 0))
        turned = jnp.where(low, pltpu.roll(moved, 8 - span, 0), pltpu.roll(moved, span, 0))
        return jnp.maximum(kept, turned)

    panels = ((0, 0), (1, 0), (1, 1))

    @pl.when(h == 0)
    def _():
        acc_s[...] = jnp.zeros_like(acc_s) if part == 0 else before[...]
        for at, (half, panel) in enumerate(panels):
            rowpos = (half * 8 + y) * SHARD + lax.broadcasted_iota(jnp.int32, (PANEL, SHARD), 1)
            rowstart = jnp.where(rowpos >= n1, n1, jnp.where(rowpos >= n0, n0, 0))
            kpos = panel * PANEL + lax.broadcasted_iota(jnp.int32, (PANEL, SHARD), 0)
            seen = (kpos <= rowpos) & (kpos >= rowstart)
            bias_s[at] = jnp.where(seen, 0.0, NEG_FILL)

    for j in range(16):
        pos = (j % 8) * 2 + jnp.where(xl == j // 8, 0, 1)
        shard = k_ref[pl.ds(pl.multiple_of(pos * SHARD, SHARD), SHARD), :]
        k_s[j * SHARD : (j + 1) * SHARD, :HEAD_DIM] = shard
        k_s[j * SHARD : (j + 1) * SHARD, HEAD_DIM:] = shard
    for g in range(GROUP):
        rows = slice(g * SHARD, (g + 1) * SHARD)
        own = q_own[:, g * HEAD_DIM : (g + 1) * HEAD_DIM].astype(jnp.float32)
        recv = q_recv[:, g * HEAD_DIM : (g + 1) * HEAD_DIM].astype(jnp.float32)
        for half in range(2):
            scaled = jnp.where(xl == half, own, recv) * EXP2_SCALE
            high = scaled.astype(jnp.bfloat16)
            q_s[half, rows, :HEAD_DIM] = high
            q_s[half, rows, HEAD_DIM:] = (scaled - high.astype(jnp.float32)).astype(jnp.bfloat16)

    def scores(item):
        pair, at = divmod(item, 3)
        half, panel = panels[at]
        slots[at][...] = lax.dot_general(
            k_s[panel * PANEL : (panel + 1) * PANEL, :],
            q_s[half, pair * 2 * SHARD : (pair + 1) * 2 * SHARD, :],
            (((1,), (1,)), ((), ())),
            preferred_element_type=jnp.float32,
        )

    def absorb(item):
        pair, at = divmod(item, 3)
        half, panel = panels[at]
        for o in range(2):
            cols = slice(o * SHARD, (o + 1) * SHARD)
            g = pair * 2 + o
            blks = []
            for b in range(PANEL // BLOCK):
                rows = slice(b * BLOCK, (b + 1) * BLOCK)
                s = slots[at][rows, cols] + bias_s[at, rows, :]
                slots[at][rows, cols] = s
                blks.append(jnp.max(s.reshape(BLOCK // 8, 8, SHARD), axis=0))
            top = tree(jnp.maximum, blks)
            for w in range(PANEL // BLOCK // 8):
                v = [blks[w * 8 + i] for i in FOLDED]
                for span in (4, 2, 1):
                    v = [fold(v[2 * i], v[2 * i + 1], span) for i in range(len(v) // 2)]
                bm_s[half, g, panel * 2 + w] = v[0]
            if panel == 1:
                m_old = m_s[half, g]
                top = jnp.maximum(m_old, top)
            e = jnp.exp2(slots[at][:, cols].reshape(PANEL // 8, 8, SHARD) - top[None])
            total = tree(jnp.add, [e[b] for b in range(PANEL // 8)])
            if panel == 1:
                total = total + l_s[half, g] * jnp.exp2(m_old - top)
            l_s[half, g] = total
            m_s[half, g] = top

    scores(0)
    for item in range(3 * GROUP // 2):
        if item + 1 < 3 * GROUP // 2:
            scores(item + 1)
        absorb(item)

    for half in range(2):
        for g in range(GROUP):
            m = m_s[half, g]
            top = jnp.max(m, axis=0, keepdims=True)
            total = jnp.sum(l_s[half, g] * jnp.exp2(m - top), axis=0, keepdims=True)
            lse = top + jnp.log2(total)
            for panel in range(half + 1):
                bm = bm_s[half, g, panel * 2 : panel * 2 + 2].reshape(NUM_BLOCKS // 2, SHARD)
                gap = bm - lse
                for i in range(2):
                    held = jnp.where(left if i == 0 else ~left, gap, NEG_FILL)
                    best = jnp.exp2(jnp.max(held, axis=1, keepdims=True))
                    col = half * 8 + (part * PART_KV + h) * 2 + i
                    acc_s[panel] += jnp.where(lane == col, best, 0.0)

    @pl.when(h == PART_KV - 1)
    def _():
        if part == 0:
            out_ref[...] = acc_s[...]
            return
        raw = acc_s[...].reshape(NUM_BLOCKS, 128)
        norm = raw / jnp.sum(raw, axis=0, keepdims=True)
        high = norm.astype(jnp.bfloat16).astype(jnp.float32)
        parts = jnp.concatenate([high, norm - high, jnp.zeros((64, 128), jnp.float32)], axis=0)
        mine = parts.T[:16, :].astype(jnp.bfloat16)
        for to in range(16):
            out_ref[to * 48 : to * 48 + 32, :] = gates[...]
            out_ref[to * 48 + 32 : to * 48 + 48, :] = mine


def attention_part(part, scalars, q, q_recv, keys, *rest):
    kw = GROUP * HEAD_DIM
    sums = (2, NUM_BLOCKS // 2, 128)
    if part == 0:
        out, out_type = sums, jnp.float32
        more = []
    else:
        out, out_type = (16 * 48, 128), jnp.bfloat16
        more = [
            pl.BlockSpec((32, 128), lambda h, sc: (0, 0)),
            pl.BlockSpec(sums, lambda h, sc: (0, 0, 0)),
            pl.BlockSpec(memory_space=pl.ANY),
        ]
    own = LOCAL_KV // PART_KV
    return pl.pallas_call(
        functools.partial(attention_kernel, part),
        out_shape=jax.ShapeDtypeStruct(out, out_type),
        grid_spec=pltpu.PrefetchScalarGridSpec(
            num_scalar_prefetch=1,
            grid=(PART_KV,),
            in_specs=[
                pl.BlockSpec((SHARD, kw), lambda h, sc: (0, (sc[2] * own + part) * PART_KV + h)),
                pl.BlockSpec((SHARD, kw), lambda h, sc: (0, h)),
                pl.BlockSpec((16 * SHARD, HEAD_DIM), lambda h, sc: (0, h)),
                *more,
            ],
            out_specs=pl.BlockSpec(out, lambda h, sc: (0,) * len(out)),
            scratch_shapes=[
                pltpu.VMEM((3, PANEL, SHARD), jnp.float32),
                pltpu.VMEM((2 * PANEL, 2 * HEAD_DIM), jnp.bfloat16),
                pltpu.VMEM((2, GROUP * SHARD, 2 * HEAD_DIM), jnp.bfloat16),
                *[pltpu.VMEM((PANEL, 2 * SHARD), jnp.float32) for _ in range(3)],
                pltpu.VMEM((2, GROUP, 8, SHARD), jnp.float32),
                pltpu.VMEM((2, GROUP, 8, SHARD), jnp.float32),
                pltpu.VMEM((2, GROUP, 4, 8, SHARD), jnp.float32),
                pltpu.VMEM((2, NUM_BLOCKS // 2, 128), jnp.float32),
            ],
        ),
        compiler_params=pltpu.CompilerParams(
            dimension_semantics=("arbitrary",), vmem_limit_bytes=56 * 1024 * 1024
        ),
        cost_estimate=pl.CostEstimate(
            flops=2 * 16 * 128 * 128 * 3072, bytes_accessed=2 << 20, transcendentals=6 << 20
        ),
        name=f"attention_{part}",
    )(scalars, q, q_recv, keys, *rest)


def gate_grads_kernel(target, gates, out_ref):
    left = lax.broadcasted_iota(jnp.int32, (NUM_BLOCKS, GATE_DIM), 1) < GATE_DIM // 2
    row = lax.broadcasted_iota(jnp.int32, (NUM_BLOCKS, NUM_BLOCKS), 0)
    causal = lax.broadcasted_iota(jnp.int32, (NUM_BLOCKS, NUM_BLOCKS), 1) <= row
    scale = 1.0 / GATE_DIM**0.5

    def product(grad, other):
        high = grad.astype(jnp.bfloat16)
        low = (grad - high.astype(jnp.float32)).astype(jnp.bfloat16)
        total = jnp.dot(high, other, preferred_element_type=jnp.float32)
        total = total + jnp.dot(low, other, preferred_element_type=jnp.float32)
        return (total * scale).astype(jnp.bfloat16).astype(jnp.float32)

    heads = range(KV_HEADS)
    logits = [
        lax.dot_general(
            gates[g],
            gates[KV_HEADS + g],
            (((1,), (1,)), ((), ())),
            preferred_element_type=jnp.float32,
        )
        for g in heads
    ]
    logits = jnp.where(causal[None], jnp.stack(logits) * scale, NEG_FILL)
    weights = jnp.exp(logits - jnp.max(logits, axis=2, keepdims=True))
    weights = jnp.where(causal[None], weights, 0.0)
    prob = weights / jnp.sum(weights, axis=2, keepdims=True)
    grad = jnp.where(causal[None], prob - target[...], 0.0)
    turned = [grad[g].T for g in heads]
    of_q = [product(grad[g], gates[KV_HEADS + g]) for g in heads]
    of_k = [product(turned[g], gates[g]) for g in heads]
    half = GATE_DIM // 2
    for g in heads:
        first = jnp.where(left, of_q[g], pltpu.roll(of_k[g], half, 1)).astype(jnp.bfloat16)
        second = jnp.where(left, pltpu.roll(of_q[g], half, 1), of_k[g]).astype(jnp.bfloat16)
        for to in range(4):
            at = (g * 4 + to) * NUM_BLOCKS
            out_ref[at : at + NUM_BLOCKS, :] = first if to % 2 == 0 else second


def weight_grads_kernel(pooled, grads, out_ref):
    depth = 4 * NUM_BLOCKS
    rows = pooled.shape[0] // 8
    total = jnp.zeros((rows, GATE_DIM), jnp.float32)
    for z in range(8):
        total = total + jnp.dot(
            pooled[z * rows : (z + 1) * rows, :],
            grads[z * depth : (z + 1) * depth, :],
            preferred_element_type=jnp.float32,
        )
    rows_k = rows // 9
    hq, hk = rows_k * 4, rows_k // 2
    of_q, of_k = total[: 2 * hq], total[2 * hq :]
    left = lax.broadcasted_iota(jnp.int32, (hq, GATE_DIM), 1) < GATE_DIM // 2
    half = GATE_DIM // 2
    top = jnp.where(left, of_q[:hq], pltpu.roll(of_q[hq:], half, 1)).astype(jnp.bfloat16)
    low = jnp.where(left[:hk], pltpu.roll(of_k[:hk], half, 1), of_k[hk:]).astype(jnp.bfloat16)
    for z in range(8):
        out_ref[z, :hq, :] = top
        out_ref[z, hq:, :] = low


def assemble_kernel(sc, own, other, out_q, out_k):
    hq, hk = out_q.shape[0] // 2, out_k.shape[0] // 2
    half = GATE_DIM // 2
    left = lax.broadcasted_iota(jnp.int32, (hq + hk, GATE_DIM), 1) < half
    first = sc[0] == 0
    for z in range(KV_HEADS):
        cols = slice(z * GATE_DIM, (z + 1) * GATE_DIM)
        mine, theirs = own[z].astype(jnp.float32), other[z].astype(jnp.float32)
        core0 = jnp.where(first, mine, theirs)
        core1 = jnp.where(first, theirs, mine)
        upper = jnp.where(left, core0, pltpu.roll(core1, half, 1)).astype(jnp.bfloat16)
        lower = jnp.where(left, pltpu.roll(core0, half, 1), core1).astype(jnp.bfloat16)
        out_q[:hq, cols] = upper[:hq]
        out_q[hq:, cols] = lower[:hq]
        out_k[:hk, cols] = upper[hq:]
        out_k[hk:, cols] = lower[hq:]


def in_vmem(kernel, out_shape, name, mib, *args):
    spec = pl.BlockSpec(memory_space=pltpu.VMEM)
    return pl.pallas_call(
        kernel,
        out_shape=out_shape,
        in_specs=[spec] * len(args),
        out_specs=spec,
        compiler_params=pltpu.CompilerParams(vmem_limit_bytes=mib * 1024 * 1024),
        name=name,
    )(*args)


def assembled(co, own, other, rows_q, rows_k):
    width = KV_HEADS * GATE_DIM
    return pl.pallas_call(
        assemble_kernel,
        out_shape=(
            jax.ShapeDtypeStruct((rows_q, width), jnp.bfloat16),
            jax.ShapeDtypeStruct((rows_k, width), jnp.bfloat16),
        ),
        in_specs=[pl.BlockSpec(memory_space=pltpu.SMEM)]
        + [pl.BlockSpec(memory_space=pltpu.VMEM)] * 2,
        out_specs=(pl.BlockSpec(memory_space=pltpu.VMEM),) * 2,
        compiler_params=pltpu.CompilerParams(vmem_limit_bytes=8 * 1024 * 1024),
        name="assembled",
    )(co.astype(jnp.int32).reshape(1), own, other)


def ordered(own, other, index):
    return jnp.where(index == 0, jnp.stack([own, other]), jnp.stack([other, own]))


def shards(queries, keys, doc_ids, gate_query_weight, gate_key_weight):
    xl, y = lax.axis_index("xl"), lax.axis_index("y")
    co, xh = lax.axis_index("co"), lax.axis_index("xh")
    q, k, doc = queries[0], keys[0], doc_ids[0]
    half_kw, half_qw = k.shape[1] // 2, q.shape[1] // 2

    with jax.named_scope("keys"):
        k_mine = lax.dynamic_slice_in_dim(k, xl * half_kw, half_kw, 1)
        k_other = lax.dynamic_slice_in_dim(k, (1 - xl) * half_kw, half_kw, 1)
        k_recv = lax.ppermute(k_other, "xl", SWAP)
        kk = jnp.concatenate([k_mine, k_recv])
        part_kw, part_qw = half_kw // 2, half_qw // 2
        first = jnp.broadcast_to(kk[None, :, :part_kw], (8, kk.shape[0], part_kw))
        first = lax.all_to_all(first, "y", split_axis=0, concat_axis=0, tiled=True)
        second = lax.all_gather(kk[:, part_kw:], "y", axis=0, tiled=True)
        keys_of = (first.reshape(-1, part_kw), second)
        q_recv = [
            lax.ppermute(
                lax.dynamic_slice_in_dim(q, (1 - xl) * half_qw + part * part_qw, part_qw, 1),
                "xl",
                SWAP,
            )
            for part in range(2)
        ]

    with jax.named_scope("pool"):
        pool_q = (
            jnp.sum(q.reshape(2, BLOCK, -1), axis=1, dtype=jnp.float32) / BLOCK
        ).astype(jnp.bfloat16)
        pool_k = jnp.max(k.reshape(2, BLOCK, -1), axis=1)
        mine = jnp.concatenate([pool_q.reshape(2, 16, -1), pool_k.reshape(2, 16, -1)], axis=2)
        pooled = lax.all_to_all(
            mine.transpose(1, 0, 2), CTX_AXES, split_axis=0, concat_axis=0, tiled=True
        ).reshape(NUM_BLOCKS, -1)
    rows_q = gate_query_weight.shape[0]
    rows_k = gate_key_weight.shape[0]
    pooled_q, pooled_k = pooled[:, :rows_q], pooled[:, rows_q:]

    with jax.named_scope("gates"):
        part = jnp.concatenate(
            [
                jnp.dot(pooled_q, gate_query_weight, preferred_element_type=jnp.float32),
                jnp.dot(pooled_k, gate_key_weight, preferred_element_type=jnp.float32),
            ],
            axis=1,
        )
        parts = lax.all_to_all(
            part.reshape(16, 2, -1), CTX_AXES, split_axis=0, concat_axis=0, tiled=True
        )
        gates_mine = jnp.sum(parts, axis=0).astype(jnp.bfloat16)
        gates_mine = gates_mine.reshape(2, 16, GATE_DIM).transpose(1, 0, 2).reshape(32, GATE_DIM)

    with jax.named_scope("pooled_all"):
        pair = ordered(pooled, lax.ppermute(pooled, "co", SWAP), co)
        quad = ordered(pair, lax.ppermute(pair, "xh", SWAP), xh)
        quad = quad.reshape(4 * NUM_BLOCKS, -1).T
        pooled_all = lax.all_gather(quad, "z", axis=0, tiled=True)

    with jax.named_scope("targets"):
        scalars = jnp.stack(
            [
                jnp.sum((doc < 1).astype(jnp.int32)),
                jnp.sum((doc < 2).astype(jnp.int32)),
                xl.astype(jnp.int32),
                y.astype(jnp.int32),
            ]
        )
        sums = attention_part(0, scalars, q, q_recv[0], keys_of[0])
        mine = attention_part(1, scalars, q, q_recv[1], keys_of[1], gates_mine, sums, quad)
        both = lax.all_to_all(mine, CTX_AXES, split_axis=0, concat_axis=0, tiled=True)
        both = both.reshape(16, 48, 128)

    with jax.named_scope("gate_grads"):
        gates = both[:, :32].reshape(16, 16, 2, GATE_DIM).transpose(1, 0, 2, 3)
        target = both[:, 32:, :NUM_BLOCKS].astype(jnp.float32)
        target = target + both[:, 32:, NUM_BLOCKS : 2 * NUM_BLOCKS].astype(jnp.float32)
        target = target.reshape(2, 8, 2, LOCAL_KV, 2, NUM_BLOCKS).transpose(0, 3, 2, 1, 4, 5)
        grads = in_vmem(
            gate_grads_kernel,
            jax.ShapeDtypeStruct((32 * NUM_BLOCKS, GATE_DIM), jnp.bfloat16),
            "gate_grads",
            16,
            target.reshape(KV_HEADS, NUM_BLOCKS, NUM_BLOCKS),
            gates.reshape(16, NUM_BLOCKS, GATE_DIM),
        )
        grads = lax.all_to_all(grads, SEQ_AXES, split_axis=0, concat_axis=0, tiled=True)

    with jax.named_scope("weight_grads"):
        pieces = in_vmem(
            weight_grads_kernel,
            jax.ShapeDtypeStruct((8, (rows_q + rows_k) // 2, GATE_DIM), jnp.bfloat16),
            "weight_grads",
            16,
            pooled_all,
            grads,
        )
        pieces = lax.all_to_all(pieces, "z", split_axis=0, concat_axis=0, tiled=True)
        out_q, out_k = assembled(co, pieces, lax.ppermute(pieces, "co", SWAP), rows_q, rows_k)
    return out_q, out_k


def solution(mesh):
    split = Mesh(mesh.devices.reshape(8, 2, 2, 2, 8), (*SEQ_AXES, *CTX_AXES))
    in_specs = (
        P(SEQ_AXES, CTX_AXES, None),
        P(SEQ_AXES, CTX_AXES, None),
        P(SEQ_AXES, None),
        P(CTX_AXES, None),
        P(CTX_AXES, None),
    )
    out_specs = (P(CTX_AXES, None), P(CTX_AXES, None))
    return jax.shard_map(
        shards, mesh=split, in_specs=in_specs, out_specs=out_specs, check_vma=False
    )
```

```python
import math

import jax
import jax.numpy as jnp
from jax import lax
from jax.experimental import pallas as pl
from jax.experimental.pallas import tpu as pltpu
from jax.sharding import Mesh, PartitionSpec as P

HEADS = 64
KV_HEADS = 8
GROUP = 8
HEAD_DIM = 128
GATE_DIM = 128
BLOCK = 64
SHARD = 128
PANEL = 1024
FOLDED = [0, 4, 2, 6, 1, 5, 3, 7]
LOCAL_KV = 4
Z_STEP = 2
NUM_BLOCKS = 32
SEQ_AXES = ("z", "xh", "co")
CTX_AXES = ("xl", "y")
SWAP = [(0, 1), (1, 0)]
NEG_FILL = -1e30
EXP2_SCALE = math.log2(math.e) / math.sqrt(HEAD_DIM)


def tree(op, parts):
    while len(parts) > 1:
        parts = [op(a, b) for a, b in zip(parts[::2], parts[1::2], strict=True)]
    return parts[0]


def attention_kernel(
    sc, q_own, q_recv, k_ref, gates, after, out_ref, bias_s, k_s, q_s, s0, s1, s2, m_s, l_s, bm_s, acc_s
):
    h = pl.program_id(0)
    n0, n1, xl, y = sc[0], sc[1], sc[2], sc[3]
    slots = (s0, s1, s2)
    sub = lax.broadcasted_iota(jnp.int32, (8, SHARD), 0)
    lane = lax.broadcasted_iota(jnp.int32, (NUM_BLOCKS // 2, 128), 1)
    left = lane < BLOCK

    def fold(first, second, span):
        low = (sub & span) == 0
        kept = jnp.where(low, first, second)
        moved = jnp.where(low, second, first)
        if span == 4:
            return jnp.maximum(kept, pltpu.roll(moved, 4, 0))
        turned = jnp.where(low, pltpu.roll(moved, 8 - span, 0), pltpu.roll(moved, span, 0))
        return jnp.maximum(kept, turned)

    panels = ((0, 0), (1, 0), (1, 1))

    @pl.when(h == 0)
    def _():
        acc_s[...] = jnp.zeros_like(acc_s)
        for at, (half, panel) in enumerate(panels):
            rowpos = (half * 8 + y) * SHARD + lax.broadcasted_iota(jnp.int32, (PANEL, SHARD), 1)
            rowstart = jnp.where(rowpos >= n1, n1, jnp.where(rowpos >= n0, n0, 0))
            kpos = panel * PANEL + lax.broadcasted_iota(jnp.int32, (PANEL, SHARD), 0)
            seen = (kpos <= rowpos) & (kpos >= rowstart)
            bias_s[at] = jnp.where(seen, 0.0, NEG_FILL)

    for j in range(16):
        pos = (j % 8) * 2 + jnp.where(xl == j // 8, 0, 1)
        shard = k_ref[pl.ds(pl.multiple_of(pos * SHARD, SHARD), SHARD), :]
        k_s[j * SHARD : (j + 1) * SHARD, :HEAD_DIM] = shard
        k_s[j * SHARD : (j + 1) * SHARD, HEAD_DIM:] = shard
    for g in range(GROUP):
        rows = slice(g * SHARD, (g + 1) * SHARD)
        own = q_own[:, g * HEAD_DIM : (g + 1) * HEAD_DIM].astype(jnp.float32)
        recv = q_recv[:, g * HEAD_DIM : (g + 1) * HEAD_DIM].astype(jnp.float32)
        for half in range(2):
            scaled = jnp.where(xl == half, own, recv) * EXP2_SCALE
            high = scaled.astype(jnp.bfloat16)
            q_s[half, rows, :HEAD_DIM] = high
            q_s[half, rows, HEAD_DIM:] = (scaled - high.astype(jnp.float32)).astype(jnp.bfloat16)

    def scores(item):
        pair, at = divmod(item, 3)
        half, panel = panels[at]
        slots[at][...] = lax.dot_general(
            k_s[panel * PANEL : (panel + 1) * PANEL, :],
            q_s[half, pair * 2 * SHARD : (pair + 1) * 2 * SHARD, :],
            (((1,), (1,)), ((), ())),
            preferred_element_type=jnp.float32,
        )

    def absorb(item):
        pair, at = divmod(item, 3)
        half, panel = panels[at]
        for o in range(2):
            cols = slice(o * SHARD, (o + 1) * SHARD)
            g = pair * 2 + o
            blks = []
            for b in range(PANEL // BLOCK):
                rows = slice(b * BLOCK, (b + 1) * BLOCK)
                s = slots[at][rows, cols] + bias_s[at, rows, :]
                slots[at][rows, cols] = s
                blks.append(jnp.max(s.reshape(BLOCK // 8, 8, SHARD), axis=0))
            top = tree(jnp.maximum, blks)
            for w in range(PANEL // BLOCK // 8):
                v = [blks[w * 8 + i] for i in FOLDED]
                for span in (4, 2, 1):
                    v = [fold(v[2 * i], v[2 * i + 1], span) for i in range(len(v) // 2)]
                bm_s[half, g, panel * 2 + w] = v[0]
            if panel == 1:
                m_old = m_s[half, g]
                top = jnp.maximum(m_old, top)
            e = jnp.exp2(slots[at][:, cols].reshape(PANEL // 8, 8, SHARD) - top[None])
            total = tree(jnp.add, [e[b] for b in range(PANEL // 8)])
            if panel == 1:
                total = total + l_s[half, g] * jnp.exp2(m_old - top)
            l_s[half, g] = total
            m_s[half, g] = top

    scores(0)
    for item in range(3 * GROUP // 2):
        if item + 1 < 3 * GROUP // 2:
            scores(item + 1)
        absorb(item)

    for half in range(2):
        for g in range(GROUP):
            m = m_s[half, g]
            top = jnp.max(m, axis=0, keepdims=True)
            total = jnp.sum(l_s[half, g] * jnp.exp2(m - top), axis=0, keepdims=True)
            lse = top + jnp.log2(total)
            for panel in range(half + 1):
                bm = bm_s[half, g, panel * 2 : panel * 2 + 2].reshape(NUM_BLOCKS // 2, SHARD)
                gap = bm - lse
                for i in range(2):
                    held = jnp.where(left if i == 0 else ~left, gap, NEG_FILL)
                    best = jnp.exp2(jnp.max(held, axis=1, keepdims=True))
                    col = half * 8 + h * 2 + i
                    acc_s[panel] += jnp.where(lane == col, best, 0.0)

    @pl.when(h == LOCAL_KV - 1)
    def _():
        raw = acc_s[...].reshape(NUM_BLOCKS, 128)
        norm = raw / jnp.sum(raw, axis=0, keepdims=True)
        high = norm.astype(jnp.bfloat16).astype(jnp.float32)
        parts = jnp.concatenate([high, norm - high, jnp.zeros((64, 128), jnp.float32)], axis=0)
        mine = parts.T[:16, :].astype(jnp.bfloat16)
        for to in range(16):
            out_ref[to * 48 : to * 48 + 32, :] = gates[...]
            out_ref[to * 48 + 32 : to * 48 + 48, :] = mine


def attention_targets(scalars, q, q_recv, k_all, gates, after):
    kw = GROUP * HEAD_DIM
    return pl.pallas_call(
        attention_kernel,
        out_shape=jax.ShapeDtypeStruct((16 * 48, 128), jnp.bfloat16),
        grid_spec=pltpu.PrefetchScalarGridSpec(
            num_scalar_prefetch=1,
            grid=(LOCAL_KV,),
            in_specs=[
                pl.BlockSpec((SHARD, kw), lambda h, sc: (0, sc[2] * LOCAL_KV + h)),
                pl.BlockSpec((SHARD, kw), lambda h, sc: (0, h)),
                pl.BlockSpec((16 * SHARD, HEAD_DIM), lambda h, sc: (0, h)),
                pl.BlockSpec((32, 128), lambda h, sc: (0, 0)),
                pl.BlockSpec(memory_space=pl.ANY),
            ],
            out_specs=pl.BlockSpec((16 * 48, 128), lambda h, sc: (0, 0)),
            scratch_shapes=[
                pltpu.VMEM((3, PANEL, SHARD), jnp.float32),
                pltpu.VMEM((2 * PANEL, 2 * HEAD_DIM), jnp.bfloat16),
                pltpu.VMEM((2, GROUP * SHARD, 2 * HEAD_DIM), jnp.bfloat16),
                *[pltpu.VMEM((PANEL, 2 * SHARD), jnp.float32) for _ in range(3)],
                pltpu.VMEM((2, GROUP, 8, SHARD), jnp.float32),
                pltpu.VMEM((2, GROUP, 8, SHARD), jnp.float32),
                pltpu.VMEM((2, GROUP, 4, 8, SHARD), jnp.float32),
                pltpu.VMEM((2, NUM_BLOCKS // 2, 128), jnp.float32),
            ],
        ),
        compiler_params=pltpu.CompilerParams(
            dimension_semantics=("arbitrary",), vmem_limit_bytes=56 * 1024 * 1024
        ),
        cost_estimate=pl.CostEstimate(
            flops=2 * 32 * 128 * 128 * 3072, bytes_accessed=4 << 20, transcendentals=12 << 20
        ),
        name="attention_targets",
    )(scalars, q, q_recv, k_all, gates, after)


def gate_grads_kernel(target, gates, out_ref):
    left = lax.broadcasted_iota(jnp.int32, (NUM_BLOCKS, GATE_DIM), 1) < GATE_DIM // 2
    row = lax.broadcasted_iota(jnp.int32, (NUM_BLOCKS, NUM_BLOCKS), 0)
    causal = lax.broadcasted_iota(jnp.int32, (NUM_BLOCKS, NUM_BLOCKS), 1) <= row
    scale = 1.0 / GATE_DIM**0.5

    def product(grad, other):
        high = grad.astype(jnp.bfloat16)
        low = (grad - high.astype(jnp.float32)).astype(jnp.bfloat16)
        total = jnp.dot(high, other, preferred_element_type=jnp.float32)
        total = total + jnp.dot(low, other, preferred_element_type=jnp.float32)
        return (total * scale).astype(jnp.bfloat16).astype(jnp.float32)

    heads = range(KV_HEADS)
    logits = [
        lax.dot_general(
            gates[g],
            gates[KV_HEADS + g],
            (((1,), (1,)), ((), ())),
            preferred_element_type=jnp.float32,
        )
        for g in heads
    ]
    logits = jnp.where(causal[None], jnp.stack(logits) * scale, NEG_FILL)
    weights = jnp.exp(logits - jnp.max(logits, axis=2, keepdims=True))
    weights = jnp.where(causal[None], weights, 0.0)
    prob = weights / jnp.sum(weights, axis=2, keepdims=True)
    grad = jnp.where(causal[None], prob - target[...], 0.0)
    turned = [grad[g].T for g in heads]
    of_q = [product(grad[g], gates[KV_HEADS + g]) for g in heads]
    of_k = [product(turned[g], gates[g]) for g in heads]
    half = GATE_DIM // 2
    for g in heads:
        first = jnp.where(left, of_q[g], pltpu.roll(of_k[g], half, 1)).astype(jnp.bfloat16)
        second = jnp.where(left, pltpu.roll(of_q[g], half, 1), of_k[g]).astype(jnp.bfloat16)
        for to in range(4):
            at = (g * 4 + to) * NUM_BLOCKS
            out_ref[at : at + NUM_BLOCKS, :] = first if to % 2 == 0 else second


def weight_grads_kernel(pooled, grads, out_ref, total_s):
    step = pl.program_id(0)
    depth = 4 * NUM_BLOCKS
    rows = total_s.shape[0]
    total = sum(
        jnp.dot(
            pooled[z * rows : (z + 1) * rows, :],
            grads[z * depth : (z + 1) * depth, :],
            preferred_element_type=jnp.float32,
        )
        for z in range(Z_STEP)
    )

    @pl.when(step == 0)
    def _():
        total_s[...] = total

    @pl.when(step > 0)
    def _():
        total_s[...] += total

    @pl.when(step == 8 // Z_STEP - 1)
    def _():
        pack_weight_grads(total_s[...], out_ref)


def pack_weight_grads(total, out_ref):
    rows = total.shape[0]
    rows_k = rows // 9
    hq, hk = rows_k * 4, rows_k // 2
    of_q, of_k = total[: 2 * hq], total[2 * hq :]
    left = lax.broadcasted_iota(jnp.int32, (hq, GATE_DIM), 1) < GATE_DIM // 2
    half = GATE_DIM // 2
    top = jnp.where(left, of_q[:hq], pltpu.roll(of_q[hq:], half, 1)).astype(jnp.bfloat16)
    low = jnp.where(left[:hk], pltpu.roll(of_k[:hk], half, 1), of_k[hk:]).astype(jnp.bfloat16)
    for z in range(8):
        out_ref[z, :hq, :] = top
        out_ref[z, hq:, :] = low


def assemble_kernel(sc, own, other, out_q, out_k):
    hq, hk = out_q.shape[0] // 2, out_k.shape[0] // 2
    half = GATE_DIM // 2
    left = lax.broadcasted_iota(jnp.int32, (hq + hk, GATE_DIM), 1) < half
    first = sc[0] == 0
    for z in range(KV_HEADS):
        cols = slice(z * GATE_DIM, (z + 1) * GATE_DIM)
        mine, theirs = own[z].astype(jnp.float32), other[z].astype(jnp.float32)
        core0 = jnp.where(first, mine, theirs)
        core1 = jnp.where(first, theirs, mine)
        upper = jnp.where(left, core0, pltpu.roll(core1, half, 1)).astype(jnp.bfloat16)
        lower = jnp.where(left, pltpu.roll(core0, half, 1), core1).astype(jnp.bfloat16)
        out_q[:hq, cols] = upper[:hq]
        out_q[hq:, cols] = lower[:hq]
        out_k[:hk, cols] = upper[hq:]
        out_k[hk:, cols] = lower[hq:]


def in_vmem(kernel, out_shape, name, mib, *args):
    spec = pl.BlockSpec(memory_space=pltpu.VMEM)
    return pl.pallas_call(
        kernel,
        out_shape=out_shape,
        in_specs=[spec] * len(args),
        out_specs=spec,
        compiler_params=pltpu.CompilerParams(vmem_limit_bytes=mib * 1024 * 1024),
        name=name,
    )(*args)


def assembled(co, own, other, rows_q, rows_k):
    width = KV_HEADS * GATE_DIM
    return pl.pallas_call(
        assemble_kernel,
        out_shape=(
            jax.ShapeDtypeStruct((rows_q, width), jnp.bfloat16),
            jax.ShapeDtypeStruct((rows_k, width), jnp.bfloat16),
        ),
        in_specs=[pl.BlockSpec(memory_space=pltpu.SMEM)]
        + [pl.BlockSpec(memory_space=pltpu.VMEM)] * 2,
        out_specs=(pl.BlockSpec(memory_space=pltpu.VMEM),) * 2,
        compiler_params=pltpu.CompilerParams(vmem_limit_bytes=8 * 1024 * 1024),
        name="assembled",
    )(co.astype(jnp.int32).reshape(1), own, other)


def weight_grads(pooled_all, grads, rows):
    return pl.pallas_call(
        weight_grads_kernel,
        out_shape=jax.ShapeDtypeStruct((8, rows // 2, GATE_DIM), jnp.bfloat16),
        grid=(8 // Z_STEP,),
        in_specs=[
            pl.BlockSpec((Z_STEP * rows, 4 * NUM_BLOCKS), lambda i: (i, 0)),
            pl.BlockSpec((Z_STEP * 4 * NUM_BLOCKS, GATE_DIM), lambda i: (i, 0)),
        ],
        out_specs=pl.BlockSpec((8, rows // 2, GATE_DIM), lambda i: (0, 0, 0)),
        scratch_shapes=[pltpu.VMEM((rows, GATE_DIM), jnp.float32)],
        compiler_params=pltpu.CompilerParams(
            dimension_semantics=("arbitrary",), vmem_limit_bytes=56 * 1024 * 1024
        ),
        name="weight_grads",
    )(pooled_all, grads)


def ordered(own, other, index):
    return jnp.where(index == 0, jnp.stack([own, other]), jnp.stack([other, own]))


def shards(queries, keys, doc_ids, gate_query_weight, gate_key_weight):
    xl, y = lax.axis_index("xl"), lax.axis_index("y")
    co, xh = lax.axis_index("co"), lax.axis_index("xh")
    q, k, doc = queries[0], keys[0], doc_ids[0]
    half_kw, half_qw = k.shape[1] // 2, q.shape[1] // 2

    with jax.named_scope("keys"):
        k_mine = lax.dynamic_slice_in_dim(k, xl * half_kw, half_kw, 1)
        k_other = lax.dynamic_slice_in_dim(k, (1 - xl) * half_kw, half_kw, 1)
        k_recv = lax.ppermute(k_other, "xl", SWAP)
        k_all = lax.all_gather(jnp.concatenate([k_mine, k_recv]), "y", axis=0, tiled=True)
        q_other = lax.dynamic_slice_in_dim(q, (1 - xl) * half_qw, half_qw, 1)
        q_recv = lax.ppermute(q_other, "xl", SWAP)

    with jax.named_scope("pool"):
        pool_q = (
            jnp.sum(q.reshape(2, BLOCK, -1), axis=1, dtype=jnp.float32) / BLOCK
        ).astype(jnp.bfloat16)
        pool_k = jnp.max(k.reshape(2, BLOCK, -1), axis=1)
        mine = jnp.concatenate([pool_q.reshape(2, 16, -1), pool_k.reshape(2, 16, -1)], axis=2)
        pooled = lax.all_to_all(
            mine.transpose(1, 0, 2), CTX_AXES, split_axis=0, concat_axis=0, tiled=True
        ).reshape(NUM_BLOCKS, -1)
    rows_q = gate_query_weight.shape[0]
    rows_k = gate_key_weight.shape[0]
    pooled_q, pooled_k = pooled[:, :rows_q], pooled[:, rows_q:]

    with jax.named_scope("gates"):
        part = jnp.concatenate(
            [
                jnp.dot(pooled_q, gate_query_weight, preferred_element_type=jnp.float32),
                jnp.dot(pooled_k, gate_key_weight, preferred_element_type=jnp.float32),
            ],
            axis=1,
        )
        parts = lax.all_to_all(
            part.reshape(16, 2, -1), CTX_AXES, split_axis=0, concat_axis=0, tiled=True
        )
        gates_mine = jnp.sum(parts, axis=0).astype(jnp.bfloat16)
        gates_mine = gates_mine.reshape(2, 16, GATE_DIM).transpose(1, 0, 2).reshape(32, GATE_DIM)

    with jax.named_scope("pooled_all"):
        pair = ordered(pooled, lax.ppermute(pooled, "co", SWAP), co)
        quad = ordered(pair, lax.ppermute(pair, "xh", SWAP), xh)
        quad = quad.reshape(4 * NUM_BLOCKS, -1).T
        pooled_all = lax.all_gather(quad, "z", axis=0, tiled=True)

    with jax.named_scope("targets"):
        scalars = jnp.stack(
            [
                jnp.sum((doc < 1).astype(jnp.int32)),
                jnp.sum((doc < 2).astype(jnp.int32)),
                xl.astype(jnp.int32),
                y.astype(jnp.int32),
            ]
        )
        mine = attention_targets(scalars, q, q_recv, k_all, gates_mine, quad)
        both = lax.all_to_all(mine, CTX_AXES, split_axis=0, concat_axis=0, tiled=True)
        both = both.reshape(16, 48, 128)

    with jax.named_scope("gate_grads"):
        gates = both[:, :32].reshape(16, 16, 2, GATE_DIM).transpose(1, 0, 2, 3)
        target = both[:, 32:, :NUM_BLOCKS].astype(jnp.float32)
        target = target + both[:, 32:, NUM_BLOCKS : 2 * NUM_BLOCKS].astype(jnp.float32)
        target = target.reshape(2, 8, 2, LOCAL_KV, 2, NUM_BLOCKS).transpose(0, 3, 2, 1, 4, 5)
        grads = in_vmem(
            gate_grads_kernel,
            jax.ShapeDtypeStruct((32 * NUM_BLOCKS, GATE_DIM), jnp.bfloat16),
            "gate_grads",
            16,
            target.reshape(KV_HEADS, NUM_BLOCKS, NUM_BLOCKS),
            gates.reshape(16, NUM_BLOCKS, GATE_DIM),
        )
        grads = lax.all_to_all(grads, SEQ_AXES, split_axis=0, concat_axis=0, tiled=True)

    with jax.named_scope("weight_grads"):
        pieces = weight_grads(pooled_all, grads, rows_q + rows_k)
        pieces = lax.all_to_all(pieces, "z", split_axis=0, concat_axis=0, tiled=True)
        out_q, out_k = assembled(co, pieces, lax.ppermute(pieces, "co", SWAP), rows_q, rows_k)
    return out_q, out_k


def solution(mesh):
    split = Mesh(mesh.devices.reshape(8, 2, 2, 2, 8), (*SEQ_AXES, *CTX_AXES))
    in_specs = (
        P(SEQ_AXES, CTX_AXES, None),
        P(SEQ_AXES, CTX_AXES, None),
        P(SEQ_AXES, None),
        P(CTX_AXES, None),
        P(CTX_AXES, None),
    )
    out_specs = (P(CTX_AXES, None), P(CTX_AXES, None))
    return jax.shard_map(
        shards, mesh=split, in_specs=in_specs, out_specs=out_specs, check_vma=False
    )
```

```python
import math

import jax
import jax.numpy as jnp
from jax import lax
from jax.experimental import pallas as pl
from jax.experimental.pallas import tpu as pltpu
from jax.sharding import Mesh, PartitionSpec as P

HEADS = 64
KV_HEADS = 8
GROUP = 8
HEAD_DIM = 128
GATE_DIM = 128
BLOCK = 64
SHARD = 128
PANEL = 1024
FOLDED = [0, 4, 2, 6, 1, 5, 3, 7]
LOCAL_KV = 4
NUM_BLOCKS = 32
SEQ_AXES = ("z", "xh", "co")
CTX_AXES = ("xl", "y")
SWAP = [(0, 1), (1, 0)]
NEG_FILL = -1e30
EXP2_SCALE = math.log2(math.e) / math.sqrt(HEAD_DIM)


def tree(op, parts):
    while len(parts) > 1:
        parts = [op(a, b) for a, b in zip(parts[::2], parts[1::2], strict=True)]
    return parts[0]


def attention_kernel(
    sc, q_own, q_recv, k_ref, gates, after, out_ref, bias_s, k_s, q_s, s0, s1, s2, m_s, l_s, bm_s, acc_s
):
    h = pl.program_id(0)
    n0, n1, xl, y = sc[0], sc[1], sc[2], sc[3]
    slots = (s0, s1, s2)
    sub = lax.broadcasted_iota(jnp.int32, (8, SHARD), 0)
    lane = lax.broadcasted_iota(jnp.int32, (NUM_BLOCKS // 2, 128), 1)
    left = lane < BLOCK

    def fold(first, second, span):
        low = (sub & span) == 0
        kept = jnp.where(low, first, second)
        moved = jnp.where(low, second, first)
        if span == 4:
            return jnp.maximum(kept, pltpu.roll(moved, 4, 0))
        turned = jnp.where(low, pltpu.roll(moved, 8 - span, 0), pltpu.roll(moved, span, 0))
        return jnp.maximum(kept, turned)

    panels = ((0, 0), (1, 0), (1, 1))

    @pl.when(h == 0)
    def _():
        acc_s[...] = jnp.zeros_like(acc_s)
        for at, (half, panel) in enumerate(panels):
            rowpos = (half * 8 + y) * SHARD + lax.broadcasted_iota(jnp.int32, (PANEL, SHARD), 1)
            rowstart = jnp.where(rowpos >= n1, n1, jnp.where(rowpos >= n0, n0, 0))
            kpos = panel * PANEL + lax.broadcasted_iota(jnp.int32, (PANEL, SHARD), 0)
            seen = (kpos <= rowpos) & (kpos >= rowstart)
            bias_s[at] = jnp.where(seen, 0.0, NEG_FILL)

    for j in range(16):
        pos = (j % 8) * 2 + jnp.where(xl == j // 8, 0, 1)
        shard = k_ref[pl.ds(pl.multiple_of(pos * SHARD, SHARD), SHARD), :]
        k_s[j * SHARD : (j + 1) * SHARD, :HEAD_DIM] = shard
        k_s[j * SHARD : (j + 1) * SHARD, HEAD_DIM:] = shard
    for g in range(GROUP):
        rows = slice(g * SHARD, (g + 1) * SHARD)
        own = q_own[:, g * HEAD_DIM : (g + 1) * HEAD_DIM].astype(jnp.float32)
        recv = q_recv[:, g * HEAD_DIM : (g + 1) * HEAD_DIM].astype(jnp.float32)
        for half in range(2):
            scaled = jnp.where(xl == half, own, recv) * EXP2_SCALE
            high = scaled.astype(jnp.bfloat16)
            q_s[half, rows, :HEAD_DIM] = high
            q_s[half, rows, HEAD_DIM:] = (scaled - high.astype(jnp.float32)).astype(jnp.bfloat16)

    def scores(item):
        pair, at = divmod(item, 3)
        half, panel = panels[at]
        slots[at][...] = lax.dot_general(
            k_s[panel * PANEL : (panel + 1) * PANEL, :],
            q_s[half, pair * 2 * SHARD : (pair + 1) * 2 * SHARD, :],
            (((1,), (1,)), ((), ())),
            preferred_element_type=jnp.float32,
        )

    def absorb(item):
        pair, at = divmod(item, 3)
        half, panel = panels[at]
        for o in range(2):
            cols = slice(o * SHARD, (o + 1) * SHARD)
            g = pair * 2 + o
            blks = []
            for b in range(PANEL // BLOCK):
                rows = slice(b * BLOCK, (b + 1) * BLOCK)
                s = slots[at][rows, cols] + bias_s[at, rows, :]
                slots[at][rows, cols] = s
                blks.append(jnp.max(s.reshape(BLOCK // 8, 8, SHARD), axis=0))
            top = tree(jnp.maximum, blks)
            for w in range(PANEL // BLOCK // 8):
                v = [blks[w * 8 + i] for i in FOLDED]
                for span in (4, 2, 1):
                    v = [fold(v[2 * i], v[2 * i + 1], span) for i in range(len(v) // 2)]
                bm_s[half, g, panel * 2 + w] = v[0]
            if panel == 1:
                m_old = m_s[half, g]
                top = jnp.maximum(m_old, top)
            e = jnp.exp2(slots[at][:, cols].reshape(PANEL // 8, 8, SHARD) - top[None])
            total = tree(jnp.add, [e[b] for b in range(PANEL // 8)])
            if panel == 1:
                total = total + l_s[half, g] * jnp.exp2(m_old - top)
            l_s[half, g] = total
            m_s[half, g] = top

    scores(0)
    for item in range(3 * GROUP // 2):
        if item + 1 < 3 * GROUP // 2:
            scores(item + 1)
        absorb(item)

    for half in range(2):
        for g in range(GROUP):
            m = m_s[half, g]
            top = jnp.max(m, axis=0, keepdims=True)
            total = jnp.sum(l_s[half, g] * jnp.exp2(m - top), axis=0, keepdims=True)
            lse = top + jnp.log2(total)
            for panel in range(half + 1):
                bm = bm_s[half, g, panel * 2 : panel * 2 + 2].reshape(NUM_BLOCKS // 2, SHARD)
                gap = bm - lse
                for i in range(2):
                    held = jnp.where(left if i == 0 else ~left, gap, NEG_FILL)
                    best = jnp.exp2(jnp.max(held, axis=1, keepdims=True))
                    col = half * 8 + h * 2 + i
                    acc_s[panel] += jnp.where(lane == col, best, 0.0)

    @pl.when(h == LOCAL_KV - 1)
    def _():
        raw = acc_s[...].reshape(NUM_BLOCKS, 128)
        norm = raw / jnp.sum(raw, axis=0, keepdims=True)
        high = norm.astype(jnp.bfloat16).astype(jnp.float32)
        parts = jnp.concatenate([high, norm - high, jnp.zeros((64, 128), jnp.float32)], axis=0)
        mine = parts.T[:16, :].astype(jnp.bfloat16)
        for to in range(16):
            out_ref[to * 48 : to * 48 + 32, :] = gates[...]
            out_ref[to * 48 + 32 : to * 48 + 48, :] = mine


def attention_targets(scalars, q, q_recv, k_all, gates, after):
    kw = GROUP * HEAD_DIM
    return pl.pallas_call(
        attention_kernel,
        out_shape=jax.ShapeDtypeStruct((16 * 48, 128), jnp.bfloat16),
        grid_spec=pltpu.PrefetchScalarGridSpec(
            num_scalar_prefetch=1,
            grid=(LOCAL_KV,),
            in_specs=[
                pl.BlockSpec((SHARD, kw), lambda h, sc: (0, sc[2] * LOCAL_KV + h)),
                pl.BlockSpec((SHARD, kw), lambda h, sc: (0, h)),
                pl.BlockSpec((16 * SHARD, HEAD_DIM), lambda h, sc: (0, h)),
                pl.BlockSpec((32, 128), lambda h, sc: (0, 0)),
                pl.BlockSpec(memory_space=pl.ANY),
            ],
            out_specs=pl.BlockSpec((16 * 48, 128), lambda h, sc: (0, 0)),
            scratch_shapes=[
                pltpu.VMEM((3, PANEL, SHARD), jnp.float32),
                pltpu.VMEM((2 * PANEL, 2 * HEAD_DIM), jnp.bfloat16),
                pltpu.VMEM((2, GROUP * SHARD, 2 * HEAD_DIM), jnp.bfloat16),
                *[pltpu.VMEM((PANEL, 2 * SHARD), jnp.float32) for _ in range(3)],
                pltpu.VMEM((2, GROUP, 8, SHARD), jnp.float32),
                pltpu.VMEM((2, GROUP, 8, SHARD), jnp.float32),
                pltpu.VMEM((2, GROUP, 4, 8, SHARD), jnp.float32),
                pltpu.VMEM((2, NUM_BLOCKS // 2, 128), jnp.float32),
            ],
        ),
        compiler_params=pltpu.CompilerParams(
            dimension_semantics=("arbitrary",), vmem_limit_bytes=56 * 1024 * 1024
        ),
        cost_estimate=pl.CostEstimate(
            flops=2 * 32 * 128 * 128 * 3072, bytes_accessed=4 << 20, transcendentals=12 << 20
        ),
        name="attention_targets",
    )(scalars, q, q_recv, k_all, gates, after)


def gate_grads_kernel(target, gates, out_ref):
    left = lax.broadcasted_iota(jnp.int32, (NUM_BLOCKS, GATE_DIM), 1) < GATE_DIM // 2
    row = lax.broadcasted_iota(jnp.int32, (NUM_BLOCKS, NUM_BLOCKS), 0)
    causal = lax.broadcasted_iota(jnp.int32, (NUM_BLOCKS, NUM_BLOCKS), 1) <= row
    scale = 1.0 / GATE_DIM**0.5

    def product(grad, other):
        high = grad.astype(jnp.bfloat16)
        low = (grad - high.astype(jnp.float32)).astype(jnp.bfloat16)
        total = jnp.dot(high, other, preferred_element_type=jnp.float32)
        total = total + jnp.dot(low, other, preferred_element_type=jnp.float32)
        return (total * scale).astype(jnp.bfloat16).astype(jnp.float32)

    heads = range(KV_HEADS)
    logits = [
        lax.dot_general(
            gates[g],
            gates[KV_HEADS + g],
            (((1,), (1,)), ((), ())),
            preferred_element_type=jnp.float32,
        )
        for g in heads
    ]
    logits = jnp.where(causal[None], jnp.stack(logits) * scale, NEG_FILL)
    weights = jnp.exp(logits - jnp.max(logits, axis=2, keepdims=True))
    weights = jnp.where(causal[None], weights, 0.0)
    prob = weights / jnp.sum(weights, axis=2, keepdims=True)
    grad = jnp.where(causal[None], prob - target[...], 0.0)
    turned = [grad[g].T for g in heads]
    of_q = [product(grad[g], gates[KV_HEADS + g]) for g in heads]
    of_k = [product(turned[g], gates[g]) for g in heads]
    half = GATE_DIM // 2
    for g in heads:
        first = jnp.where(left, of_q[g], pltpu.roll(of_k[g], half, 1)).astype(jnp.bfloat16)
        second = jnp.where(left, pltpu.roll(of_q[g], half, 1), of_k[g]).astype(jnp.bfloat16)
        for to in range(4):
            at = (g * 4 + to) * NUM_BLOCKS
            out_ref[at : at + NUM_BLOCKS, :] = first if to % 2 == 0 else second


def weight_grads_kernel(pooled, grads, out_ref):
    depth = 4 * NUM_BLOCKS
    rows = pooled.shape[0] // 8
    total = jnp.zeros((rows, GATE_DIM), jnp.float32)
    for z in range(8):
        total = total + jnp.dot(
            pooled[z * rows : (z + 1) * rows, :],
            grads[z * depth : (z + 1) * depth, :],
            preferred_element_type=jnp.float32,
        )
    rows_k = rows // 9
    hq, hk = rows_k * 4, rows_k // 2
    of_q, of_k = total[: 2 * hq], total[2 * hq :]
    left = lax.broadcasted_iota(jnp.int32, (hq, GATE_DIM), 1) < GATE_DIM // 2
    half = GATE_DIM // 2
    top = jnp.where(left, of_q[:hq], pltpu.roll(of_q[hq:], half, 1)).astype(jnp.bfloat16)
    low = jnp.where(left[:hk], pltpu.roll(of_k[:hk], half, 1), of_k[hk:]).astype(jnp.bfloat16)
    for z in range(8):
        out_ref[z, :hq, :] = top
        out_ref[z, hq:, :] = low


def assemble_kernel(sc, own, other, out_q, out_k):
    hq, hk = out_q.shape[0] // 2, out_k.shape[0] // 2
    half = GATE_DIM // 2
    left = lax.broadcasted_iota(jnp.int32, (hq + hk, GATE_DIM), 1) < half
    first = sc[0] == 0
    for z in range(KV_HEADS):
        cols = slice(z * GATE_DIM, (z + 1) * GATE_DIM)
        mine, theirs = own[z].astype(jnp.float32), other[z].astype(jnp.float32)
        core0 = jnp.where(first, mine, theirs)
        core1 = jnp.where(first, theirs, mine)
        upper = jnp.where(left, core0, pltpu.roll(core1, half, 1)).astype(jnp.bfloat16)
        lower = jnp.where(left, pltpu.roll(core0, half, 1), core1).astype(jnp.bfloat16)
        out_q[:hq, cols] = upper[:hq]
        out_q[hq:, cols] = lower[:hq]
        out_k[:hk, cols] = upper[hq:]
        out_k[hk:, cols] = lower[hq:]


def in_vmem(kernel, out_shape, name, mib, *args):
    spec = pl.BlockSpec(memory_space=pltpu.VMEM)
    return pl.pallas_call(
        kernel,
        out_shape=out_shape,
        in_specs=[spec] * len(args),
        out_specs=spec,
        compiler_params=pltpu.CompilerParams(vmem_limit_bytes=mib * 1024 * 1024),
        name=name,
    )(*args)


def assembled(co, own, other, rows_q, rows_k):
    width = KV_HEADS * GATE_DIM
    return pl.pallas_call(
        assemble_kernel,
        out_shape=(
            jax.ShapeDtypeStruct((rows_q, width), jnp.bfloat16),
            jax.ShapeDtypeStruct((rows_k, width), jnp.bfloat16),
        ),
        in_specs=[pl.BlockSpec(memory_space=pltpu.SMEM)]
        + [pl.BlockSpec(memory_space=pltpu.VMEM)] * 2,
        out_specs=(pl.BlockSpec(memory_space=pltpu.VMEM),) * 2,
        compiler_params=pltpu.CompilerParams(vmem_limit_bytes=8 * 1024 * 1024),
        name="assembled",
    )(co.astype(jnp.int32).reshape(1), own, other)


def ordered(own, other, index):
    return jnp.where(index == 0, jnp.stack([own, other]), jnp.stack([other, own]))


def shards(queries, keys, doc_ids, gate_query_weight, gate_key_weight):
    xl, y = lax.axis_index("xl"), lax.axis_index("y")
    co, xh = lax.axis_index("co"), lax.axis_index("xh")
    q, k, doc = queries[0], keys[0], doc_ids[0]
    half_kw, half_qw = k.shape[1] // 2, q.shape[1] // 2

    with jax.named_scope("keys"):
        k_mine = lax.dynamic_slice_in_dim(k, xl * half_kw, half_kw, 1)
        k_other = lax.dynamic_slice_in_dim(k, (1 - xl) * half_kw, half_kw, 1)
        k_recv = lax.ppermute(k_other, "xl", SWAP)
        k_all = lax.all_gather(jnp.concatenate([k_mine, k_recv]), "y", axis=0, tiled=True)
        q_other = lax.dynamic_slice_in_dim(q, (1 - xl) * half_qw, half_qw, 1)
        q_recv = lax.ppermute(q_other, "xl", SWAP)

    with jax.named_scope("pool"):
        pool_q = (
            jnp.sum(q.reshape(2, BLOCK, -1), axis=1, dtype=jnp.float32) / BLOCK
        ).astype(jnp.bfloat16)
        pool_k = jnp.max(k.reshape(2, BLOCK, -1), axis=1)
        mine = jnp.concatenate([pool_q.reshape(2, 16, -1), pool_k.reshape(2, 16, -1)], axis=2)
        pooled = lax.all_to_all(
            mine.transpose(1, 0, 2), CTX_AXES, split_axis=0, concat_axis=0, tiled=True
        ).reshape(NUM_BLOCKS, -1)
    rows_q = gate_query_weight.shape[0]
    rows_k = gate_key_weight.shape[0]
    pooled_q, pooled_k = pooled[:, :rows_q], pooled[:, rows_q:]

    with jax.named_scope("gates"):
        part = jnp.concatenate(
            [
                jnp.dot(pooled_q, gate_query_weight, preferred_element_type=jnp.float32),
                jnp.dot(pooled_k, gate_key_weight, preferred_element_type=jnp.float32),
            ],
            axis=1,
        )
        parts = lax.all_to_all(
            part.reshape(16, 2, -1), CTX_AXES, split_axis=0, concat_axis=0, tiled=True
        )
        gates_mine = jnp.sum(parts, axis=0).astype(jnp.bfloat16)
        gates_mine = gates_mine.reshape(2, 16, GATE_DIM).transpose(1, 0, 2).reshape(32, GATE_DIM)

    with jax.named_scope("pooled_all"):
        pair = ordered(pooled, lax.ppermute(pooled, "co", SWAP), co)
        quad = ordered(pair, lax.ppermute(pair, "xh", SWAP), xh)
        quad = quad.reshape(4 * NUM_BLOCKS, -1).T
        pooled_all = lax.all_gather(quad, "z", axis=0, tiled=True)

    with jax.named_scope("targets"):
        scalars = jnp.stack(
            [
                jnp.sum((doc < 1).astype(jnp.int32)),
                jnp.sum((doc < 2).astype(jnp.int32)),
                xl.astype(jnp.int32),
                y.astype(jnp.int32),
            ]
        )
        mine = attention_targets(scalars, q, q_recv, k_all, gates_mine, quad)
        both = lax.all_to_all(mine, CTX_AXES, split_axis=0, concat_axis=0, tiled=True)
        both = both.reshape(16, 48, 128)

    with jax.named_scope("gate_grads"):
        gates = both[:, :32].reshape(16, 16, 2, GATE_DIM).transpose(1, 0, 2, 3)
        target = both[:, 32:, :NUM_BLOCKS].astype(jnp.float32)
        target = target + both[:, 32:, NUM_BLOCKS : 2 * NUM_BLOCKS].astype(jnp.float32)
        target = target.reshape(2, 8, 2, LOCAL_KV, 2, NUM_BLOCKS).transpose(0, 3, 2, 1, 4, 5)
        grads = in_vmem(
            gate_grads_kernel,
            jax.ShapeDtypeStruct((32 * NUM_BLOCKS, GATE_DIM), jnp.bfloat16),
            "gate_grads",
            16,
            target.reshape(KV_HEADS, NUM_BLOCKS, NUM_BLOCKS),
            gates.reshape(16, NUM_BLOCKS, GATE_DIM),
        )
        grads = lax.all_to_all(grads, SEQ_AXES, split_axis=0, concat_axis=0, tiled=True)

    with jax.named_scope("weight_grads"):
        pieces = in_vmem(
            weight_grads_kernel,
            jax.ShapeDtypeStruct((8, (rows_q + rows_k) // 2, GATE_DIM), jnp.bfloat16),
            "weight_grads",
            16,
            pooled_all,
            grads,
        )
        pieces = lax.all_to_all(pieces, "z", split_axis=0, concat_axis=0, tiled=True)
        out_q, out_k = assembled(co, pieces, lax.ppermute(pieces, "co", SWAP), rows_q, rows_k)
    return out_q, out_k


def solution(mesh):
    split = Mesh(mesh.devices.reshape(8, 2, 2, 2, 8), (*SEQ_AXES, *CTX_AXES))
    in_specs = (
        P(SEQ_AXES, CTX_AXES, None),
        P(SEQ_AXES, CTX_AXES, None),
        P(SEQ_AXES, None),
        P(CTX_AXES, None),
        P(CTX_AXES, None),
    )
    out_specs = (P(CTX_AXES, None), P(CTX_AXES, None))
    return jax.shard_map(
        shards, mesh=split, in_specs=in_specs, out_specs=out_specs, check_vma=False
    )
```

```python
import math

import jax
import jax.numpy as jnp
from jax import lax
from jax.experimental import pallas as pl
from jax.experimental.pallas import tpu as pltpu
from jax.sharding import Mesh, PartitionSpec as P

HEADS = 64
KV_HEADS = 8
GROUP = 8
HEAD_DIM = 128
GATE_DIM = 128
BLOCK = 64
SHARD = 128
PANEL = 1024
FOLDED = [0, 4, 2, 6, 1, 5, 3, 7]
LOCAL_KV = 4
NUM_BLOCKS = 32
SEQ_AXES = ("z", "xh", "co")
CTX_AXES = ("xl", "y")
SWAP = [(0, 1), (1, 0)]
NEG_FILL = -1e30
EXP2_SCALE = math.log2(math.e) / math.sqrt(HEAD_DIM)


def tree(op, parts):
    while len(parts) > 1:
        parts = [op(a, b) for a, b in zip(parts[::2], parts[1::2], strict=True)]
    return parts[0]


def attention_kernel(
    sc, q_own, q_recv, k_ref, gates, after, out_ref, bias_s, k_s, q_s, s0, s1, s2, m_s, l_s, bm_s, acc_s
):
    h = pl.program_id(0)
    n0, n1, xl, y = sc[0], sc[1], sc[2], sc[3]
    slots = (s0, s1, s2)
    sub = lax.broadcasted_iota(jnp.int32, (8, SHARD), 0)
    lane = lax.broadcasted_iota(jnp.int32, (NUM_BLOCKS // 2, 128), 1)
    left = lane < BLOCK

    def fold(first, second, span):
        low = (sub & span) == 0
        kept = jnp.where(low, first, second)
        moved = jnp.where(low, second, first)
        if span == 4:
            return jnp.maximum(kept, pltpu.roll(moved, 4, 0))
        turned = jnp.where(low, pltpu.roll(moved, 8 - span, 0), pltpu.roll(moved, span, 0))
        return jnp.maximum(kept, turned)

    panels = ((0, 0), (1, 0), (1, 1))

    @pl.when(h == 0)
    def _():
        acc_s[...] = jnp.zeros_like(acc_s)
        for at, (half, panel) in enumerate(panels):
            rowpos = (half * 8 + y) * SHARD + lax.broadcasted_iota(jnp.int32, (PANEL, SHARD), 1)
            rowstart = jnp.where(rowpos >= n1, n1, jnp.where(rowpos >= n0, n0, 0))
            kpos = panel * PANEL + lax.broadcasted_iota(jnp.int32, (PANEL, SHARD), 0)
            seen = (kpos <= rowpos) & (kpos >= rowstart)
            bias_s[at] = jnp.where(seen, 0.0, NEG_FILL)

    for j in range(16):
        pos = (j % 8) * 2 + jnp.where(xl == j // 8, 0, 1)
        shard = k_ref[pl.ds(pl.multiple_of(pos * SHARD, SHARD), SHARD), :]
        k_s[j * SHARD : (j + 1) * SHARD, :HEAD_DIM] = shard
        k_s[j * SHARD : (j + 1) * SHARD, HEAD_DIM:] = shard
    for g in range(GROUP):
        rows = slice(g * SHARD, (g + 1) * SHARD)
        own = q_own[:, g * HEAD_DIM : (g + 1) * HEAD_DIM].astype(jnp.float32)
        recv = q_recv[:, g * HEAD_DIM : (g + 1) * HEAD_DIM].astype(jnp.float32)
        for half in range(2):
            scaled = jnp.where(xl == half, own, recv) * EXP2_SCALE
            high = scaled.astype(jnp.bfloat16)
            q_s[half, rows, :HEAD_DIM] = high
            q_s[half, rows, HEAD_DIM:] = (scaled - high.astype(jnp.float32)).astype(jnp.bfloat16)

    def scores(item):
        pair, at = divmod(item, 3)
        half, panel = panels[at]
        slots[at][...] = lax.dot_general(
            k_s[panel * PANEL : (panel + 1) * PANEL, :],
            q_s[half, pair * 2 * SHARD : (pair + 1) * 2 * SHARD, :],
            (((1,), (1,)), ((), ())),
            preferred_element_type=jnp.float32,
        )

    def absorb(item):
        pair, at = divmod(item, 3)
        half, panel = panels[at]
        for o in range(2):
            cols = slice(o * SHARD, (o + 1) * SHARD)
            g = pair * 2 + o
            blks = []
            for b in range(PANEL // BLOCK):
                rows = slice(b * BLOCK, (b + 1) * BLOCK)
                s = slots[at][rows, cols] + bias_s[at, rows, :]
                slots[at][rows, cols] = s
                blks.append(jnp.max(s.reshape(BLOCK // 8, 8, SHARD), axis=0))
            top = tree(jnp.maximum, blks)
            for w in range(PANEL // BLOCK // 8):
                v = [blks[w * 8 + i] for i in FOLDED]
                for span in (4, 2, 1):
                    v = [fold(v[2 * i], v[2 * i + 1], span) for i in range(len(v) // 2)]
                bm_s[half, g, panel * 2 + w] = v[0]
            if panel == 1:
                m_old = m_s[half, g]
                top = jnp.maximum(m_old, top)
            e = jnp.exp2(slots[at][:, cols].reshape(PANEL // 8, 8, SHARD) - top[None])
            total = tree(jnp.add, [e[b] for b in range(PANEL // 8)])
            if panel == 1:
                total = total + l_s[half, g] * jnp.exp2(m_old - top)
            l_s[half, g] = total
            m_s[half, g] = top

    scores(0)
    for item in range(3 * GROUP // 2):
        if item + 1 < 3 * GROUP // 2:
            scores(item + 1)
        absorb(item)

    for half in range(2):
        for g in range(GROUP):
            m = m_s[half, g]
            top = jnp.max(m, axis=0, keepdims=True)
            total = jnp.sum(l_s[half, g] * jnp.exp2(m - top), axis=0, keepdims=True)
            lse = top + jnp.log2(total)
            for panel in range(half + 1):
                bm = bm_s[half, g, panel * 2 : panel * 2 + 2].reshape(NUM_BLOCKS // 2, SHARD)
                gap = bm - lse
                for i in range(2):
                    held = jnp.where(left if i == 0 else ~left, gap, NEG_FILL)
                    best = jnp.exp2(jnp.max(held, axis=1, keepdims=True))
                    col = half * 8 + h * 2 + i
                    acc_s[panel] += jnp.where(lane == col, best, 0.0)

    @pl.when(h == LOCAL_KV - 1)
    def _():
        raw = acc_s[...].reshape(NUM_BLOCKS, 128)
        norm = raw / jnp.sum(raw, axis=0, keepdims=True)
        high = norm.astype(jnp.bfloat16).astype(jnp.float32)
        parts = jnp.concatenate([high, norm - high, jnp.zeros((64, 128), jnp.float32)], axis=0)
        mine = parts.T[:16, :].astype(jnp.bfloat16)
        for to in range(16):
            out_ref[to * 48 : to * 48 + 32, :] = gates[...]
            out_ref[to * 48 + 32 : to * 48 + 48, :] = mine


def attention_targets(scalars, q, q_recv, k_all, gates, after):
    kw = GROUP * HEAD_DIM
    return pl.pallas_call(
        attention_kernel,
        out_shape=jax.ShapeDtypeStruct((16 * 48, 128), jnp.bfloat16),
        grid_spec=pltpu.PrefetchScalarGridSpec(
            num_scalar_prefetch=1,
            grid=(LOCAL_KV,),
            in_specs=[
                pl.BlockSpec((SHARD, kw), lambda h, sc: (0, sc[2] * LOCAL_KV + h)),
                pl.BlockSpec((SHARD, kw), lambda h, sc: (0, h)),
                pl.BlockSpec((16 * SHARD, HEAD_DIM), lambda h, sc: (0, h)),
                pl.BlockSpec((32, 128), lambda h, sc: (0, 0)),
                pl.BlockSpec(memory_space=pl.ANY),
            ],
            out_specs=pl.BlockSpec((16 * 48, 128), lambda h, sc: (0, 0)),
            scratch_shapes=[
                pltpu.VMEM((3, PANEL, SHARD), jnp.float32),
                pltpu.VMEM((2 * PANEL, 2 * HEAD_DIM), jnp.bfloat16),
                pltpu.VMEM((2, GROUP * SHARD, 2 * HEAD_DIM), jnp.bfloat16),
                *[pltpu.VMEM((PANEL, 2 * SHARD), jnp.float32) for _ in range(3)],
                pltpu.VMEM((2, GROUP, 8, SHARD), jnp.float32),
                pltpu.VMEM((2, GROUP, 8, SHARD), jnp.float32),
                pltpu.VMEM((2, GROUP, 4, 8, SHARD), jnp.float32),
                pltpu.VMEM((2, NUM_BLOCKS // 2, 128), jnp.float32),
            ],
        ),
        compiler_params=pltpu.CompilerParams(
            dimension_semantics=("arbitrary",), vmem_limit_bytes=56 * 1024 * 1024
        ),
        cost_estimate=pl.CostEstimate(
            flops=2 * 32 * 128 * 128 * 3072, bytes_accessed=4 << 20, transcendentals=12 << 20
        ),
        name="attention_targets",
    )(scalars, q, q_recv, k_all, gates, after)


def gate_grads_kernel(target, gates, out_ref):
    left = lax.broadcasted_iota(jnp.int32, (NUM_BLOCKS, GATE_DIM), 1) < GATE_DIM // 2
    row = lax.broadcasted_iota(jnp.int32, (NUM_BLOCKS, NUM_BLOCKS), 0)
    causal = lax.broadcasted_iota(jnp.int32, (NUM_BLOCKS, NUM_BLOCKS), 1) <= row
    scale = 1.0 / GATE_DIM**0.5

    def product(grad, other):
        high = grad.astype(jnp.bfloat16)
        low = (grad - high.astype(jnp.float32)).astype(jnp.bfloat16)
        total = jnp.dot(high, other, preferred_element_type=jnp.float32)
        total = total + jnp.dot(low, other, preferred_element_type=jnp.float32)
        return (total * scale).astype(jnp.bfloat16).astype(jnp.float32)

    heads = range(KV_HEADS)
    logits = [
        lax.dot_general(
            gates[g],
            gates[KV_HEADS + g],
            (((1,), (1,)), ((), ())),
            preferred_element_type=jnp.float32,
        )
        for g in heads
    ]
    logits = jnp.where(causal[None], jnp.stack(logits) * scale, NEG_FILL)
    weights = jnp.exp(logits - jnp.max(logits, axis=2, keepdims=True))
    weights = jnp.where(causal[None], weights, 0.0)
    prob = weights / jnp.sum(weights, axis=2, keepdims=True)
    grad = jnp.where(causal[None], prob - target[...], 0.0)
    turned = [grad[g].T for g in heads]
    of_q = [product(grad[g], gates[KV_HEADS + g]) for g in heads]
    of_k = [product(turned[g], gates[g]) for g in heads]
    half = GATE_DIM // 2
    for g in heads:
        first = jnp.where(left, of_q[g], pltpu.roll(of_k[g], half, 1)).astype(jnp.bfloat16)
        second = jnp.where(left, pltpu.roll(of_q[g], half, 1), of_k[g]).astype(jnp.bfloat16)
        for to in range(4):
            at = (g * 4 + to) * NUM_BLOCKS
            out_ref[at : at + NUM_BLOCKS, :] = first if to % 2 == 0 else second


def weight_grads_kernel(pooled_hbm, grads, out_ref, pooled, sems):
    depth = 4 * NUM_BLOCKS
    rows = pooled.shape[0] // 8
    copies = []
    for z in range(8):
        part = pl.ds(z * rows, rows)
        copies.append(pltpu.make_async_copy(pooled_hbm.at[part], pooled.at[part], sems.at[z]))
        copies[z].start()
    total = jnp.zeros((rows, GATE_DIM), jnp.float32)
    for z in range(8):
        copies[z].wait()
        total = total + jnp.dot(
            pooled[z * rows : (z + 1) * rows, :],
            grads[z * depth : (z + 1) * depth, :],
            preferred_element_type=jnp.float32,
        )
    rows_k = rows // 9
    hq, hk = rows_k * 4, rows_k // 2
    of_q, of_k = total[: 2 * hq], total[2 * hq :]
    left = lax.broadcasted_iota(jnp.int32, (hq, GATE_DIM), 1) < GATE_DIM // 2
    half = GATE_DIM // 2
    top = jnp.where(left, of_q[:hq], pltpu.roll(of_q[hq:], half, 1)).astype(jnp.bfloat16)
    low = jnp.where(left[:hk], pltpu.roll(of_k[:hk], half, 1), of_k[hk:]).astype(jnp.bfloat16)
    for z in range(8):
        out_ref[z, :hq, :] = top
        out_ref[z, hq:, :] = low


def assemble_kernel(sc, own, other, out_q, out_k):
    hq, hk = out_q.shape[0] // 2, out_k.shape[0] // 2
    half = GATE_DIM // 2
    left = lax.broadcasted_iota(jnp.int32, (hq + hk, GATE_DIM), 1) < half
    first = sc[0] == 0
    for z in range(KV_HEADS):
        cols = slice(z * GATE_DIM, (z + 1) * GATE_DIM)
        mine, theirs = own[z].astype(jnp.float32), other[z].astype(jnp.float32)
        core0 = jnp.where(first, mine, theirs)
        core1 = jnp.where(first, theirs, mine)
        upper = jnp.where(left, core0, pltpu.roll(core1, half, 1)).astype(jnp.bfloat16)
        lower = jnp.where(left, pltpu.roll(core0, half, 1), core1).astype(jnp.bfloat16)
        out_q[:hq, cols] = upper[:hq]
        out_q[hq:, cols] = lower[:hq]
        out_k[:hk, cols] = upper[hq:]
        out_k[hk:, cols] = lower[hq:]


def in_vmem(kernel, out_shape, name, mib, *args):
    spec = pl.BlockSpec(memory_space=pltpu.VMEM)
    return pl.pallas_call(
        kernel,
        out_shape=out_shape,
        in_specs=[spec] * len(args),
        out_specs=spec,
        compiler_params=pltpu.CompilerParams(vmem_limit_bytes=mib * 1024 * 1024),
        name=name,
    )(*args)


def assembled(co, own, other, rows_q, rows_k):
    width = KV_HEADS * GATE_DIM
    return pl.pallas_call(
        assemble_kernel,
        out_shape=(
            jax.ShapeDtypeStruct((rows_q, width), jnp.bfloat16),
            jax.ShapeDtypeStruct((rows_k, width), jnp.bfloat16),
        ),
        in_specs=[pl.BlockSpec(memory_space=pltpu.SMEM)]
        + [pl.BlockSpec(memory_space=pltpu.VMEM)] * 2,
        out_specs=(pl.BlockSpec(memory_space=pltpu.VMEM),) * 2,
        compiler_params=pltpu.CompilerParams(vmem_limit_bytes=8 * 1024 * 1024),
        name="assembled",
    )(co.astype(jnp.int32).reshape(1), own, other)


def ordered(own, other, index):
    return jnp.where(index == 0, jnp.stack([own, other]), jnp.stack([other, own]))


def shards(queries, keys, doc_ids, gate_query_weight, gate_key_weight):
    xl, y = lax.axis_index("xl"), lax.axis_index("y")
    co, xh = lax.axis_index("co"), lax.axis_index("xh")
    q, k, doc = queries[0], keys[0], doc_ids[0]
    half_kw, half_qw = k.shape[1] // 2, q.shape[1] // 2

    with jax.named_scope("keys"):
        k_mine = lax.dynamic_slice_in_dim(k, xl * half_kw, half_kw, 1)
        k_other = lax.dynamic_slice_in_dim(k, (1 - xl) * half_kw, half_kw, 1)
        k_recv = lax.ppermute(k_other, "xl", SWAP)
        k_all = lax.all_gather(jnp.concatenate([k_mine, k_recv]), "y", axis=0, tiled=True)
        q_other = lax.dynamic_slice_in_dim(q, (1 - xl) * half_qw, half_qw, 1)
        q_recv = lax.ppermute(q_other, "xl", SWAP)

    with jax.named_scope("pool"):
        pool_q = (
            jnp.sum(q.reshape(2, BLOCK, -1), axis=1, dtype=jnp.float32) / BLOCK
        ).astype(jnp.bfloat16)
        pool_k = jnp.max(k.reshape(2, BLOCK, -1), axis=1)
        mine = jnp.concatenate([pool_q.reshape(2, 16, -1), pool_k.reshape(2, 16, -1)], axis=2)
        pooled = lax.all_to_all(
            mine.transpose(1, 0, 2), CTX_AXES, split_axis=0, concat_axis=0, tiled=True
        ).reshape(NUM_BLOCKS, -1)
    rows_q = gate_query_weight.shape[0]
    rows_k = gate_key_weight.shape[0]
    pooled_q, pooled_k = pooled[:, :rows_q], pooled[:, rows_q:]

    with jax.named_scope("gates"):
        part = jnp.concatenate(
            [
                jnp.dot(pooled_q, gate_query_weight, preferred_element_type=jnp.float32),
                jnp.dot(pooled_k, gate_key_weight, preferred_element_type=jnp.float32),
            ],
            axis=1,
        )
        parts = lax.all_to_all(
            part.reshape(16, 2, -1), CTX_AXES, split_axis=0, concat_axis=0, tiled=True
        )
        gates_mine = jnp.sum(parts, axis=0).astype(jnp.bfloat16)
        gates_mine = gates_mine.reshape(2, 16, GATE_DIM).transpose(1, 0, 2).reshape(32, GATE_DIM)

    with jax.named_scope("pooled_all"):
        pair = ordered(pooled, lax.ppermute(pooled, "co", SWAP), co)
        quad = ordered(pair, lax.ppermute(pair, "xh", SWAP), xh)
        quad = quad.reshape(4 * NUM_BLOCKS, -1).T
        pooled_all = lax.all_gather(quad, "z", axis=0, tiled=True)

    with jax.named_scope("targets"):
        scalars = jnp.stack(
            [
                jnp.sum((doc < 1).astype(jnp.int32)),
                jnp.sum((doc < 2).astype(jnp.int32)),
                xl.astype(jnp.int32),
                y.astype(jnp.int32),
            ]
        )
        mine = attention_targets(scalars, q, q_recv, k_all, gates_mine, quad)
        both = lax.all_to_all(mine, CTX_AXES, split_axis=0, concat_axis=0, tiled=True)
        both = both.reshape(16, 48, 128)

    with jax.named_scope("gate_grads"):
        gates = both[:, :32].reshape(16, 16, 2, GATE_DIM).transpose(1, 0, 2, 3)
        target = both[:, 32:, :NUM_BLOCKS].astype(jnp.float32)
        target = target + both[:, 32:, NUM_BLOCKS : 2 * NUM_BLOCKS].astype(jnp.float32)
        target = target.reshape(2, 8, 2, LOCAL_KV, 2, NUM_BLOCKS).transpose(0, 3, 2, 1, 4, 5)
        grads = in_vmem(
            gate_grads_kernel,
            jax.ShapeDtypeStruct((32 * NUM_BLOCKS, GATE_DIM), jnp.bfloat16),
            "gate_grads",
            16,
            target.reshape(KV_HEADS, NUM_BLOCKS, NUM_BLOCKS),
            gates.reshape(16, NUM_BLOCKS, GATE_DIM),
        )
        grads = lax.all_to_all(grads, SEQ_AXES, split_axis=0, concat_axis=0, tiled=True)

    with jax.named_scope("weight_grads"):
        in_vmem_spec = pl.BlockSpec(memory_space=pltpu.VMEM)
        pieces = pl.pallas_call(
            weight_grads_kernel,
            out_shape=jax.ShapeDtypeStruct((8, (rows_q + rows_k) // 2, GATE_DIM), jnp.bfloat16),
            in_specs=[pl.BlockSpec(memory_space=pl.ANY), in_vmem_spec],
            out_specs=in_vmem_spec,
            scratch_shapes=[
                pltpu.VMEM(pooled_all.shape, jnp.bfloat16),
                pltpu.SemaphoreType.DMA((8,)),
            ],
            compiler_params=pltpu.CompilerParams(vmem_limit_bytes=56 * 1024 * 1024),
            name="weight_grads",
        )(pooled_all, grads)
        pieces = lax.all_to_all(pieces, "z", split_axis=0, concat_axis=0, tiled=True)
        out_q, out_k = assembled(co, pieces, lax.ppermute(pieces, "co", SWAP), rows_q, rows_k)
    return out_q, out_k


def solution(mesh):
    split = Mesh(mesh.devices.reshape(8, 2, 2, 2, 8), (*SEQ_AXES, *CTX_AXES))
    in_specs = (
        P(SEQ_AXES, CTX_AXES, None),
        P(SEQ_AXES, CTX_AXES, None),
        P(SEQ_AXES, None),
        P(CTX_AXES, None),
        P(CTX_AXES, None),
    )
    out_specs = (P(CTX_AXES, None), P(CTX_AXES, None))
    return jax.shard_map(
        shards, mesh=split, in_specs=in_specs, out_specs=out_specs, check_vma=False
    )
```
